256 devices in a mesh: dp: 4 (over x), seq: 64 (over y, z, core).
Axes of the slice: x: 4, y: 4, z: 8, core: 2. Of those that a mesh axis runs over, the one named last changes fastest.
Arguments:
- tokens: bfloat16 [4, 8192, 1024], P('dp', 'seq'), may hold values from -16 to 16
- qkv_weight: bfloat16 [1024, 3072], P('dp'), may hold values from -0.1875 to 0.1875
- out_gain: bfloat16 [1024], replicated, may hold values from 0.099609375 to 1.8984375
- out_grad: bfloat16 [4, 8192, 1024], P('dp', 'seq'), may hold values from -0.125 to 0.125
Outputs:
- attended: bfloat16 [4, 8192, 1024], P('dp', 'seq')
- input_grad: bfloat16 [4, 8192, 1024], P('dp', 'seq')
- weight_grad: float32 [1024, 3072], P(('dp', 'seq'))
- gain_grad: float32 [1024], replicated
The draws below stay inside these ranges and needn't reach their ends.
All inputs are finite; a program needn't handle non-finite values.
Results may differ from the reference program's by a relative error of at most 0.014.
Values may be sent and summed in bfloat16 or wider, within the bound.
No kernel may reach another device: no remote copies, remote signals or barrier semaphores. Data moves between devices by JAX's collectives and lax.ppermute only.
A program may use at most 192 MiB of HBM per device.

```python
import jax
import jax.numpy as jnp
from jax import lax

D = 1024
HEADS = 8
HEAD_DIM = 128
TOK_DEV = 128
INNER = 1024
SEQ_LEN = 8192
BATCH = 4


def raised(values, rng, source, target, shards_of, factor):
    owner, partner = [(jnp.arange(values.shape[dim]) // (values.shape[dim] // shards_of)).reshape([-1 if axis == dim else 1 for axis in range(values.ndim)]) for dim in (source, target)]
    chosen = jax.random.permutation(rng, shards_of)[partner]
    strong = (owner == chosen) | (owner == (partner + shards_of // 2) % shards_of)
    return jnp.where(strong, factor * values, values)


def levels(rng, dims, split, least, high):
    factor_of = 1.0
    for dim, parts in split:
        draws = jax.random.uniform(jax.random.fold_in(jax.random.fold_in(rng, 6), dim), (parts,), jnp.float32, least / len(split), high / len(split))
        factor_of = factor_of * jnp.repeat(jnp.exp(draws), dims[dim] // parts).reshape((-1,) + (1,) * (len(dims) - 1 - dim))
    return factor_of


def scatter_about(rng, shape, width, bound, pieces=(), dtype=jnp.bfloat16):
    array = width * jax.random.normal(rng, shape, jnp.float32)
    if pieces:
        array = array * levels(rng, shape, pieces, -0.22, 0.18)
    return jnp.clip(array, -bound, bound).astype(dtype)


def noise_with(stream_key, extent, width, limit, shards, heavy, held_as=jnp.bfloat16):
    array = width * jax.random.normal(stream_key, extent, jnp.float32)
    if shards:
        array = array * levels(stream_key, extent, shards, -0.22, 0.18)
    return jnp.clip(raised(array, jax.random.fold_in(stream_key, 3), *heavy), -limit, limit).astype(held_as)


def setup_inputs(seed: int = 0) -> dict:
    seeds = jax.random.split(jax.random.key(seed), 5)
    tokens = noise_with(seeds[0], (BATCH, SEQ_LEN, D), 1.0, 16.0, ((0, 4), (1, 64)), (1, 2, 64, 4.0))
    qkv_weight = scatter_about(seeds[1], (D, 3 * INNER), D ** -0.5, 0.1875, ((0, 4),))
    out_gain = jnp.clip(1.0 + 0.18 * jax.random.normal(seeds[2], (INNER,), jnp.float32), 0.099609375, 1.8984375).astype(jnp.bfloat16)
    out_grad = scatter_about(seeds[3], (BATCH, SEQ_LEN, INNER), 0.02, 0.125, ((0, 4), (1, 64)))
    return dict(tokens=tokens, qkv_weight=qkv_weight, out_gain=out_gain, out_grad=out_grad)


EPSILON = 1e-05
HIGH = lax.Precision.HIGHEST

def one_sequence(inputs, qkv_weight, out_gain, upstream_bf):
    blocks = SEQ_LEN // TOK_DEV
    projected = jnp.dot(inputs, qkv_weight, preferred_element_type=jnp.float32).astype(jnp.bfloat16)
    shaped = projected.astype(jnp.float32).reshape(blocks, TOK_DEV, 3, HEADS, HEAD_DIM)
    query_rows = shaped[:, :, 0]
    key_rows = shaped[:, :, 1]
    value_rows = shaped[:, :, 2]
    kv_local = jnp.einsum('nchd,nche->nhde', key_rows, value_rows)
    prefix = jnp.cumsum(kv_local, axis=0) - kv_local
    positions = jnp.arange(TOK_DEV)
    causal_mask = (positions[:, None] >= positions[None, :]).astype(jnp.float32)
    scores = (jnp.einsum('nthd,nshd->nhts', query_rows, key_rows) * causal_mask).astype(jnp.bfloat16)
    scores_wide = scores.astype(jnp.float32)
    mixed = jnp.einsum('nthd,nhde->nthe', query_rows, prefix, precision=HIGH)
    mixed = mixed + jnp.einsum('nhts,nshe->nthe', scores_wide, value_rows)
    inverse_rms = lax.rsqrt(lax.optimization_barrier(jnp.mean(mixed * mixed, axis=-1, keepdims=True)) + EPSILON)
    normed = mixed * inverse_rms
    gain_heads = out_gain.astype(jnp.float32).reshape(HEADS, HEAD_DIM)
    attended = (gain_heads * normed).astype(jnp.bfloat16).reshape(SEQ_LEN, INNER)
    upstream = upstream_bf.astype(jnp.float32).reshape(blocks, TOK_DEV, HEADS, HEAD_DIM)
    gain_part = lax.optimization_barrier(jnp.sum(upstream * normed, axis=(0, 1))).reshape(INNER)
    normed_grad = upstream * gain_heads
    mixed_grad = inverse_rms * (normed_grad - normed * lax.optimization_barrier(jnp.mean(normed_grad * normed, axis=-1, keepdims=True)))
    mixed_grad = mixed_grad.astype(jnp.bfloat16).astype(jnp.float32)
    grad_local = jnp.einsum('nthd,nthe->nhde', query_rows, mixed_grad)
    suffix = jnp.cumsum(grad_local[::-1], axis=0)[::-1] - grad_local
    score_grad = (jnp.einsum('nthe,nshe->nhts', mixed_grad, value_rows) * causal_mask).astype(jnp.bfloat16)
    score_grad = score_grad.astype(jnp.float32)
    query_grad = jnp.einsum('nhts,nshd->nthd', score_grad, key_rows)
    query_grad = query_grad + jnp.einsum('nthe,nhde->nthd', mixed_grad, prefix, precision=HIGH)
    key_grad = jnp.einsum('nhts,nthd->nshd', score_grad, query_rows)
    key_grad = key_grad + jnp.einsum('nshe,nhde->nshd', value_rows, suffix, precision=HIGH)
    value_grad = jnp.einsum('nhts,nthe->nshe', scores_wide, mixed_grad)
    value_grad = value_grad + jnp.einsum('nshd,nhde->nshe', key_rows, suffix, precision=HIGH)
    projected_grad = jnp.concatenate([query_grad.reshape(SEQ_LEN, INNER), key_grad.reshape(SEQ_LEN, INNER), value_grad.reshape(SEQ_LEN, INNER)], axis=1).astype(jnp.bfloat16)
    return (attended, projected_grad, gain_part)

def reference(tokens, qkv_weight, out_gain, out_grad):

    def per_sequence(pair):
        return one_sequence(pair[0], qkv_weight, out_gain, pair[1])
    attended, projected_grad, gain_parts = lax.map(per_sequence, (tokens, out_grad))
    flat_tokens = tokens.reshape(BATCH * SEQ_LEN, D)
    flat_grad = projected_grad.reshape(BATCH * SEQ_LEN, 3 * INNER)
    input_grad = jnp.dot(flat_grad, qkv_weight.T, preferred_element_type=jnp.float32).astype(jnp.bfloat16)
    weight_grad = jnp.dot(flat_tokens.T, flat_grad, preferred_element_type=jnp.float32) / BATCH
    gain_grad = lax.optimization_barrier(jnp.sum(gain_parts, axis=0)) / BATCH
    return (attended, input_grad.reshape(BATCH, SEQ_LEN, D), weight_grad, gain_grad)
```

```python
import jax
import jax.numpy as jnp
from jax import lax
from jax.sharding import Mesh, PartitionSpec as P

HEADS = 8
HEAD_DIM = 128
EPSILON = 1e-05
BF = jnp.bfloat16
F32 = jnp.float32

SEQ = ("yh", "yl", "zh", "zm", "zl", "c")
CUBE = ("yl", "zl", "c")
RUN = ("zh", "zm")
ALL = ("dp",) + SEQ
SWAP = [(0, 1), (1, 0)]


def swap(x, axis):
    return lax.ppermute(x, axis, SWAP)


def ordered(mine, other, axis):
    first = lax.axis_index(axis) == 0
    return jnp.where(first, jnp.stack([mine, other]), jnp.stack([other, mine]))


def dot(a, b, contract, out=F32):
    return lax.dot_general(a, b, ((contract[0], contract[1]), ((), ())), preferred_element_type=F32).astype(out)


def gather_cube(block):
    half = block.shape[1] // 2
    left, right = block[:, :half], block[:, half:]
    left = ordered(left, swap(left, "yl"), "yl")
    right = ordered(right, swap(right, "zl"), "zl")
    left_far = swap(left, "zl")
    right_far = swap(right, "yl")
    left = jnp.swapaxes(ordered(left, left_far, "zl"), 0, 1)
    right = ordered(right, right_far, "yl")
    both = jnp.concatenate([left, right], axis=-1)
    core = swap(both, "c")
    full = ordered(both, core, "c")
    return jnp.transpose(full, (1, 2, 0, 3, 4)).reshape(8 * block.shape[0], block.shape[1])


def parts3(x):
    high = x.astype(BF)
    rest = x - high.astype(F32)
    middle = rest.astype(BF)
    return high, middle, (rest - middle.astype(F32)).astype(BF)


def exchange(states, extra, backward):
    d = states.shape[-1]
    rows = 16
    def pack(s, e):
        pad = jnp.zeros((rows - 3, d), BF)
        return jnp.concatenate([s.reshape(-1, d).astype(BF), e, pad], axis=0)
    place = lax.axis_index(RUN)
    payload = pack(states, extra)
    mine = payload.astype(F32)
    total = mine
    near = jnp.zeros((2 * d, d), F32)
    for k in (1, 2, 3):
        got = lax.ppermute(payload, RUN, [(i, i ^ k) for i in range(4)]).astype(F32)
        total = total + got
        source = place ^ k
        use = (source > place) if backward else (source < place)
        near = near + jnp.where(use, got[: 2 * d], 0.0)
    term = total[2 * d : 2 * d + 3].sum(axis=0)
    both = total[:d] + total[d : 2 * d]
    far = swap(pack(both, jnp.stack(parts3(term))), "yh").astype(F32)
    yh = lax.axis_index("yh")
    cross = jnp.where((yh == 0) if backward else (yh == 1), far[:d], 0.0)
    near = near.reshape(2, d, d)
    if backward:
        state = jnp.stack([near[0] + total[d : 2 * d] + cross, near[1] + cross])
    else:
        state = jnp.stack([near[0] + cross, near[1] + total[:d] + cross])
    return state, term + far[d : d + 3].sum(axis=0)


def local(tokens, qkv_weight, out_gain, out_grad):
    replicas = lax.axis_size("dp")
    d = HEAD_DIM
    block = tokens[0]
    n, width = block.shape
    inner = out_gain.shape[0]
    depth = qkv_weight.shape[0]
    head = lax.axis_index(CUBE)
    core = lax.axis_index("c")
    dp = lax.axis_index("dp")

    everyone = gather_cube(block)

    w_head = lax.dynamic_index_in_dim(qkv_weight.reshape(depth, 3, HEADS, d), head, 2, False).reshape(depth, 3 * d)
    pieces = jnp.zeros((replicas, depth, 3 * d), BF)
    pieces = lax.dynamic_update_index_in_dim(pieces, w_head, dp, 0)
    for k in range(1, replicas):
        got = lax.ppermute(w_head, "dp", [(i, (i + k) % replicas) for i in range(replicas)])
        pieces = lax.dynamic_update_index_in_dim(pieces, got, lax.rem(dp - k + replicas, replicas), 0)
    w_cols = pieces.reshape(replicas * depth, 3 * d)

    upstream = lax.all_to_all(
        jnp.swapaxes(out_grad[0].reshape(n, HEADS, d), 0, 1), CUBE, 0, 0, tiled=True
    ).reshape(2, 4 * n, d)

    w_half = lax.dynamic_slice_in_dim(qkv_weight, core * (depth // 2), depth // 2, 0)
    w_mine = lax.all_gather(w_half, "dp", axis=0, tiled=True)
    w_other = swap(w_mine, "c")

    projected = dot(everyone, w_cols, ((1,), (0,)), BF).reshape(2, 4 * n, 3, d)
    query, key, value = projected[:, :, 0], projected[:, :, 1], projected[:, :, 2]
    kv = jnp.einsum("scd,sce->sde", key, value, preferred_element_type=F32)
    before, _ = exchange(kv, jnp.zeros((3, d), BF), False)
    before = before.astype(BF)
    rows = lax.iota(jnp.int32, 4 * n)
    causal = rows[:, None] >= rows[None, :]
    scores = jnp.where(causal, jnp.einsum("std,sud->stu", query, key, preferred_element_type=F32), 0.0).astype(BF)
    mixed = jnp.einsum("stu,sue->ste", scores, value, preferred_element_type=F32)
    mixed = mixed + jnp.einsum("std,sde->ste", query, before, preferred_element_type=F32)
    inverse_rms = lax.rsqrt(jnp.mean(mixed * mixed, axis=-1, keepdims=True) + EPSILON)
    normed = mixed * inverse_rms
    gain = lax.dynamic_slice_in_dim(out_gain, head * d, d, 0).astype(F32)
    attended_head = (gain * normed).astype(BF)
    up = upstream.astype(F32)
    gain_part = jnp.sum(up * normed, axis=(0, 1))
    normed_grad = up * gain
    mixed_grad = (
        inverse_rms * (normed_grad - normed * jnp.mean(normed_grad * normed, axis=-1, keepdims=True))
    ).astype(BF)
    grads = jnp.einsum("std,ste->sde", query, mixed_grad, preferred_element_type=F32)
    after, gain_sum = exchange(grads, jnp.stack(parts3(gain_part)), True)
    after = after.astype(BF)

    gain_rows = jnp.concatenate([jnp.stack(parts3(gain_sum)), jnp.zeros((13, d), BF)], axis=0)
    sent = jnp.concatenate(
        [attended_head.reshape(HEADS, n, d), jnp.broadcast_to(gain_rows[None], (HEADS, 16, d))], axis=1
    )
    back = lax.all_to_all(sent, CUBE, 0, 0, tiled=True)
    attended = jnp.swapaxes(back[:, :n], 0, 1).reshape(n, inner)
    gain_all = back[:, n : n + 3].astype(F32).sum(axis=1)
    gain_total = gain_all
    for k in range(1, replicas):
        gain_total = gain_total + lax.ppermute(gain_all, "dp", [(i, (i + k) % replicas) for i in range(replicas)])
    gain_grad = gain_total.reshape(inner) / replicas

    score_grad = jnp.where(
        causal, jnp.einsum("ste,sue->stu", mixed_grad, value, preferred_element_type=F32), 0.0
    ).astype(BF)
    query_grad = jnp.einsum("stu,sud->std", score_grad, key, preferred_element_type=F32)
    query_grad = query_grad + jnp.einsum("ste,sde->std", mixed_grad, before, preferred_element_type=F32)
    key_grad = jnp.einsum("stu,std->sud", score_grad, query, preferred_element_type=F32)
    key_grad = key_grad + jnp.einsum("sue,sde->sud", value, after, preferred_element_type=F32)
    value_grad = jnp.einsum("stu,ste->sue", scores, mixed_grad, preferred_element_type=F32)
    value_grad = value_grad + jnp.einsum("sud,sde->sue", key, after, preferred_element_type=F32)
    projected_grad = jnp.concatenate([query_grad, key_grad, value_grad], axis=-1).astype(BF).reshape(8 * n, 3 * d)

    home = lax.all_to_all(projected_grad.reshape(HEADS, n, 3 * d), CUBE, 0, 0, tiled=True)
    home = jnp.transpose(home.reshape(HEADS, n, 3, d), (1, 2, 0, 3)).reshape(n, 3 * inner)
    part_mine = dot(home, w_mine, ((1,), (1,)), BF).reshape(n, replicas, 1, depth // 2)
    part_other = dot(home, w_other, ((1,), (1,)), BF).reshape(n, replicas, 1, depth // 2)
    input_grad = jnp.where(
        core == 0,
        jnp.concatenate([part_mine, part_other], axis=2),
        jnp.concatenate([part_other, part_mine], axis=2),
    ).reshape(n, width)

    weight_part = dot(everyone, projected_grad, ((0,), (0,)), BF)
    shared = lax.all_to_all(weight_part.reshape(256, width // 256, 3 * d), ALL, 0, 0, tiled=True)
    shared = shared.reshape(replicas, 2, 2, 4, 2, 2, width // 256, 3, d).astype(F32)
    weight_grad = jnp.transpose(shared.sum(axis=(0, 1, 3)), (3, 4, 0, 1, 2, 5)).reshape(width // 256, 3 * inner)
    weight_grad = weight_grad / replicas
    return (attended[None], input_grad[None], weight_grad, gain_grad)


def solution(mesh):
    fine = Mesh(mesh.devices.reshape(mesh.devices.shape[0], 2, 2, 2, 2, 2, 2), ALL)
    rows = P("dp", SEQ, None)
    return jax.shard_map(
        local,
        mesh=fine,
        in_specs=(rows, P("dp", None), P(), rows),
        out_specs=(rows, rows, P(ALL, None), P()),
        check_vma=False,
    )
```

```python
import jax
import jax.numpy as jnp
from jax import lax
from jax.experimental import pallas as pl
from jax.experimental.pallas import tpu as pltpu
from jax.sharding import Mesh, PartitionSpec as P

HEADS = 8
HEAD_DIM = 128
EPSILON = 1e-05
BF = jnp.bfloat16
F32 = jnp.float32

SEQ = ("yh", "yl", "zh", "zm", "zl", "c")
CUBE = ("yl", "zl", "c")
RUN = ("zh", "zm")
ALL = ("dp",) + SEQ
NN = (((1,), (0,)), ((), ()))
NT = (((1,), (1,)), ((), ()))
TN = (((0,), (0,)), ((), ()))


def swap(x, axes, bit, count):
    return lax.ppermute(x, axes, [(i, i ^ bit) for i in range(count)])


def dot(a, b, dims):
    return lax.dot_general(a, b, dims, preferred_element_type=F32)


def together(*xs):
    return lax.optimization_barrier(xs)


def call(body, outs, *operands, flops=0, scratch=()):
    size = sum(o.size * o.dtype.itemsize for o in (*operands, *outs))
    count, total = len(operands), len(operands) + len(outs)

    def kernel(*refs):
        far, near, (sems, *rest) = refs[:total], refs[total : 2 * total], refs[2 * total :]
        loads = [pltpu.make_async_copy(far[i], near[i], sems.at[i]) for i in range(count)]
        stores = [pltpu.make_async_copy(near[i], far[i], sems.at[i]) for i in range(count, total)]
        waited, started = set(), set()

        def ready(*places):
            for i in places or range(count):
                if i not in waited:
                    loads[i].wait()
                    waited.add(i)

        def finish(*places):
            for i in places or range(len(stores)):
                if i not in started:
                    stores[i].start()
                    started.add(i)

        for load in loads:
            load.start()
        body(ready, finish, *near, *rest)
        ready()
        finish()
        for store in stores:
            store.wait()

    return pl.pallas_call(
        kernel,
        out_shape=[pltpu.HBM(o.shape, o.dtype) for o in outs],
        in_specs=[pl.BlockSpec(memory_space=pltpu.HBM)] * count,
        out_specs=[pl.BlockSpec(memory_space=pltpu.HBM)] * len(outs),
        scratch_shapes=[pltpu.VMEM(o.shape, o.dtype) for o in (*operands, *outs)]
        + [pltpu.SemaphoreType.DMA((total,))]
        + list(scratch),
        cost_estimate=pl.CostEstimate(flops=flops, bytes_accessed=size, transcendentals=0),
        compiler_params=pltpu.CompilerParams(vmem_limit_bytes=60 * 2**20),
    )(*operands)


def shape(dims, dtype):
    return jax.ShapeDtypeStruct(dims, dtype)


def slices(weight, tokens, grad):
    depth, d, half = weight.shape[0], HEAD_DIM, weight.shape[0] // 2
    n, width = tokens.shape

    def kernel(weight, tokens, grad, heads_out, half_out, b0, b1, b2, b3, head, half_near, tok, cols, sems):
        me, core = lax.axis_index(CUBE), lax.axis_index("c")
        loads = [(tokens, tok)]
        for k in range(4):
            at = pl.multiple_of(((me // 2) ^ k) * 2 * d, 2 * d)
            loads.append((grad.at[:, pl.ds(at, 2 * d)], cols.at[k]))
        for part in range(3):
            at = pl.multiple_of((part * HEADS + me) * d, d)
            loads.append((weight.at[:, pl.ds(at, d)], head.at[:, pl.ds(part * d, d)]))
        loads.append((weight.at[pl.ds(pl.multiple_of(core * half, half), half), :], half_near))
        loads = [pltpu.make_async_copy(x, y, sems.at[i]) for i, (x, y) in enumerate(loads)]
        stores = []
        for k, block in enumerate((b0, b1, b2, b3)):
            stores.append((tok, block.at[:, pl.ds(0, width)]))
            stores.append((cols.at[k], block.at[:, pl.ds(width, 2 * d)]))
        for j in range(4):
            stores.append((head, heads_out.at[pl.ds(j * depth, depth), :]))
        stores.append((half_near, half_out))
        stores = [pltpu.make_async_copy(x, y, sems.at[i + len(loads)]) for i, (x, y) in enumerate(stores)]
        for copy in loads:
            copy.start()
        for some, then in ((loads[:5], stores[:8]), (loads[5:8], stores[8:12]), (loads[8:], stores[12:])):
            for copy in some:
                copy.wait()
            for copy in then:
                copy.start()
        for copy in stores:
            copy.wait()

    outs = ((4 * depth, 3 * d), (half, weight.shape[1])) + ((n, width + 2 * d),) * 4
    near = ((depth, 3 * d), (half, weight.shape[1]), (n, width), (4, n, 2 * d))
    return pl.pallas_call(
        kernel,
        out_shape=[pltpu.HBM(o, BF) for o in outs],
        in_specs=[pl.BlockSpec(memory_space=pltpu.HBM)] * 3,
        out_specs=[pl.BlockSpec(memory_space=pltpu.HBM)] * len(outs),
        scratch_shapes=[pltpu.VMEM(o, BF) for o in near] + [pltpu.SemaphoreType.DMA((22,))],
        cost_estimate=pl.CostEstimate(flops=0, bytes_accessed=2**21, transcendentals=0),
        compiler_params=pltpu.CompilerParams(vmem_limit_bytes=60 * 2**20),
    )(weight, tokens, grad)


def project(ready, finish, w, *refs):
    pieces, (query, key, value, states, upstream) = refs[:8], refs[8:]
    n, d = pieces[0].shape[0], HEAD_DIM
    width = w.shape[0]
    me = lax.axis_index(CUBE)
    at = pl.multiple_of(width + lax.axis_index("c") * d, d)
    ready(0)
    for k in range(8):
        ready(1 + k)
        got = dot(pieces[k][:, :width], w[...], NN).astype(BF)
        rows = pl.ds(pl.multiple_of((me ^ k) * n, n), n)
        for part, ref in enumerate((query, key, value)):
            ref[rows, :] = got[:, part * d : (part + 1) * d]
        upstream[rows, :] = pieces[k][:, pl.ds(at, d)]
    finish(0, 1, 2, 4)
    half = 4 * n
    for s in range(2):
        rows = pl.ds(s * half, half)
        states[pl.ds(s * d, d), :] = dot(key[rows, :], value[rows, :], TN).astype(BF)


def below(rows):
    return lax.broadcasted_iota(jnp.int32, (rows, rows), 0) >= lax.broadcasted_iota(jnp.int32, (rows, rows), 1)


def inside(ready, finish, query, key, value, scores, intra):
    ready()
    half = query.shape[0] // 2
    keep = below(half)
    for s in range(2):
        rows = pl.ds(s * half, half)
        got = jnp.where(keep, dot(query[rows, :], key[rows, :], NT), 0.0).astype(BF)
        scores[rows, :] = got
        intra[rows, :] = dot(got, value[rows, :], NN)


def combine(ready, finish, mine, a, b, c, out):
    ready()
    d = HEAD_DIM
    total = mine[...].astype(F32) + a[...].astype(F32) + b[...].astype(F32) + c[...].astype(F32)
    out[:d, :] = (total[:d] + total[d : 2 * d]).astype(BF)
    if out.shape[0] > d:
        out[d:, :] = in_parts(jnp.sum(total[2 * d :], axis=0, keepdims=True))


def in_parts(row):
    high = row.astype(BF).astype(F32)
    middle = (row - high).astype(BF).astype(F32)
    low = row - high - middle
    place = lax.broadcasted_iota(jnp.int32, (16, row.shape[1]), 0)
    return jnp.where(place == 0, high, jnp.where(place == 1, middle, jnp.where(place == 2, low, 0.0))).astype(BF)


def states_at(mine, got, far, backward):
    d = HEAD_DIM
    place = lax.axis_index(RUN)
    total = mine[: 2 * d, :].astype(F32)
    near = jnp.zeros_like(total)
    for k, ref in enumerate(got):
        term = ref[: 2 * d, :].astype(F32)
        source = place ^ (k + 1)
        use = (source > place) if backward else (source < place)
        near = near + jnp.where(use, term, 0.0)
        total = total + term
    yh = lax.axis_index("yh")
    cross = jnp.where((yh == 0) if backward else (yh == 1), far[:d, :].astype(F32), 0.0)
    if backward:
        return near[:d] + total[d:] + cross, near[d:] + cross
    return near[:d] + cross, near[d:] + total[:d] + cross


def forward(
    ready, finish, query, intra, mine, a, b, c, far, upstream, gain, attended, mixed_grad, payload, before
):
    ready()
    d = HEAD_DIM
    half = query.shape[0] // 2
    scale = gain[:, pl.ds(pl.multiple_of(lax.axis_index(CUBE) * d, d), d)].astype(F32)
    gain_part = jnp.zeros((1, d), F32)
    for s, state in enumerate(states_at(mine, (a, b, c), far, False)):
        state = state.astype(BF)
        before[pl.ds(s * d, d), :] = state
        rows = pl.ds(s * half, half)
        mixed = intra[rows, :] + dot(query[rows, :], state, NN)
        inverse_rms = lax.rsqrt(jnp.mean(mixed * mixed, axis=-1, keepdims=True) + EPSILON)
        normed = mixed * inverse_rms
        attended[rows, :] = (scale * normed).astype(BF)
        up = upstream[rows, :].astype(F32)
        product = up * normed
        gain_part = gain_part + jnp.sum(product, axis=0, keepdims=True)
        along = jnp.mean(product * scale, axis=-1, keepdims=True)
        grad = (inverse_rms * (up * scale - normed * along)).astype(BF)
        mixed_grad[rows, :] = grad
        payload[pl.ds(s * d, d), :] = dot(query[rows, :], grad, TN).astype(BF)
    payload[2 * d :, :] = in_parts(gain_part)


def backward_inside(
    ready, finish, query, key, value, scores, mixed_grad, before, attended, sent, key_part, value_part
):
    ready()
    d = HEAD_DIM
    half = query.shape[0] // 2
    keep = below(half)
    for s in range(2):
        rows = pl.ds(s * half, half)
        grad = mixed_grad[rows, :]
        got = jnp.where(keep, dot(grad, value[rows, :], NT), 0.0).astype(BF)
        sent[rows, :d] = attended[rows, :]
        sent[rows, d:] = (dot(got, key[rows, :], NN) + dot(grad, before[pl.ds(s * d, d), :], NT)).astype(BF)
        key_part[rows, :] = dot(got, query[rows, :], TN)
        value_part[rows, :] = dot(scores[rows, :], grad, TN)


def backward_rest(ready, finish, key, value, sent, key_part, value_part, mine, a, b, c, far, late, joined):
    ready()
    d = HEAD_DIM
    n = key.shape[0] // 8
    half = 4 * n
    terms = jnp.zeros((16, d), F32)
    for ref in (mine, a, b, c):
        terms = terms + ref[2 * d :, :].astype(F32)
    gain = in_parts(jnp.sum(terms + far[d:, :].astype(F32), axis=0, keepdims=True))
    joined[:, :d] = sent[:, d:]
    for s, state in enumerate(states_at(mine, (a, b, c), far, True)):
        state = state.astype(BF)
        rows = pl.ds(s * half, half)
        key_grad = (key_part[rows, :] + dot(value[rows, :], state, NT)).astype(BF)
        value_grad = (value_part[rows, :] + dot(key[rows, :], state, NN)).astype(BF)
        joined[rows, d : 2 * d] = key_grad
        joined[rows, 2 * d :] = value_grad
        for i in range(4):
            late[s * 4 + i, :n, : 2 * d] = sent[pl.ds(s * half + i * n, n), :]
            late[s * 4 + i, :n, 2 * d : 3 * d] = key_grad[i * n : (i + 1) * n]
            late[s * 4 + i, :n, 3 * d :] = value_grad[i * n : (i + 1) * n]
    for h in range(HEADS):
        late[h, n:, :d] = gain
        late[h, n:, d:] = jnp.zeros((16, 3 * d), BF)


def weigh(ready, finish, joined, *refs):
    pieces, (out, order, turned) = refs[:8], refs[8:]
    n, width = joined.shape[0] // 8, out.shape[0]
    me = lax.axis_index(CUBE)
    ready(0)
    for k in range(8):
        order[k * n : (k + 1) * n, :] = joined[pl.ds(pl.multiple_of((me ^ k) * n, n), n), :]
    for k in range(8):
        ready(1 + k)
        turned[:, k * n : (k + 1) * n] = pieces[k][:, :width].T
    out[...] = dot(turned[...], order[...], NN).astype(BF)


def at_home(ready, finish, late, mine, other, out, attended, gains, joined):
    ready(0)
    n = out.shape[0]
    d = HEAD_DIM
    for h in range(HEADS):
        attended[:, h * d : (h + 1) * d] = late[h, :n, :d]
        joined[h] = late[h, :n, d:]
        terms = jnp.sum(late[h, n:, :d].astype(F32), axis=0, keepdims=True)
        gains[h] = jnp.broadcast_to(terms, (8, d))
    finish(1, 2)
    ready()
    rows = jnp.concatenate(
        [joined[h, :, part * d : (part + 1) * d] for part in range(3) for h in range(HEADS)], axis=1
    )
    first = dot(rows, mine[...], NT).astype(BF)
    second = dot(rows, other[...], NT).astype(BF)
    width = mine.shape[0] // 4
    even = lax.axis_index("c") == 0
    for p in range(4):
        x, y = first[:, p * width : (p + 1) * width], second[:, p * width : (p + 1) * width]
        out[:, 2 * p * width : (2 * p + 1) * width] = jnp.where(even, x, y)
        out[:, (2 * p + 1) * width : (2 * p + 2) * width] = jnp.where(even, y, x)


def add_first(ready, finish, pieces, out):
    ready()
    rows = pieces.shape[0] // 16
    for yl in range(2):
        total = sum(
            pieces[pl.ds(((dp * 2 + yh) * 2 + yl) * rows, rows), :].astype(F32) for dp in range(4) for yh in range(2)
        )
        for j in range(16):
            out[j * 8 + yl * 4 : j * 8 + yl * 4 + 4, :] = total[j * 4 : j * 4 + 4, :]


def add_up(ready, finish, pieces, g0, g1, g2, g3, weight_grad, gain_grad):
    ready()
    d = HEAD_DIM
    for low in range(4):
        total = sum(pieces[pl.ds((run * 4 + low) * 8, 8), :] for run in range(4)) / 4
        for yl in range(2):
            for part in range(3):
                at = (part * HEADS + yl * 4 + low) * d
                weight_grad[:, at : at + d] = total[yl * 4 : yl * 4 + 4, part * d : (part + 1) * d]
    for h in range(HEADS):
        gain_grad[h : h + 1, :] = sum(ref[h, :1, :] for ref in (g0, g1, g2, g3)) / 4


def local(tokens, qkv_weight, out_gain, out_grad):
    replicas = lax.axis_size("dp")
    d = HEAD_DIM
    block = tokens[0]
    n, width = block.shape
    inner = out_gain.shape[0]
    depth = qkv_weight.shape[0]

    w_heads, w_half, *blocks = slices(qkv_weight, block, out_grad[0])
    near = [swap(blocks[bit], ("yl", "zl"), bit, 4) for bit in (1, 2, 3)]
    w_cols = lax.all_to_all(w_heads, "dp", 0, 0, tiled=True)
    mine, _ = together(blocks[0], near[0])
    pieces = [x for side in [mine] + near for x in (side, swap(side, "c", 1, 2))]

    rows = 8 * n
    column, square = shape((rows, d), BF), shape((2 * d, d), BF)
    query, key, value, states, upstream = call(
        project, (column, column, column, square, column), w_cols, *pieces,
        flops=2 * rows * width * 3 * d,
    )
    w_half, _ = together(w_half, states)
    w_mine = lax.all_gather(w_half, "dp", axis=0, tiled=True)
    scores, intra = call(
        inside, (shape((rows, rows // 2), BF), shape((rows, d), F32)), query, key, value, flops=2 * rows * rows * d
    )
    got = [swap(states, RUN, bit, 4) for bit in (1, 2, 3)]
    (both,) = call(combine, (shape((d, d), BF),), states, *got)
    far = swap(both, "yh", 1, 2)
    attended_head, mixed_grad, payload, before = call(
        forward, (column, column, shape((2 * d + 16, d), BF), square),
        query, intra, states, *got, far, upstream, out_gain.reshape(1, inner), flops=4 * rows * d * d,
    )
    grads = [swap(payload, RUN, bit, 4) for bit in (1, 2, 3)]
    (both_grad,) = call(combine, (shape((d + 16, d), BF),), payload, *grads)
    mixed_grad, both_grad = together(mixed_grad, both_grad)
    sent, key_part, value_part = call(
        backward_inside, (shape((rows, 2 * d), BF), shape((rows, d), F32), shape((rows, d), F32)),
        query, key, value, scores, mixed_grad, before, attended_head, flops=4 * rows * rows * d,
    )
    far_grad = swap(both_grad, "yh", 1, 2)
    late, joined = call(
        backward_rest, (shape((HEADS, n + 16, 4 * d), BF), shape((rows, 3 * d), BF)),
        key, value, sent, key_part, value_part, payload, *grads, far_grad, flops=8 * rows * d * d,
    )
    late = lax.all_to_all(late, CUBE, 0, 0, tiled=True)
    (weight_part,) = call(
        weigh, (shape((width, 3 * d), BF),), joined, *pieces,
        flops=2 * rows * width * 3 * d,
        scratch=[pltpu.VMEM((rows, 3 * d), BF), pltpu.VMEM((width, rows), BF)],
    )
    w_mine, _ = together(w_mine, weight_part)
    w_other = swap(w_mine, "c", 1, 2)
    weight_part, _ = together(weight_part, late)
    sums = lax.all_to_all(weight_part, ("dp", "yh", "yl"), 0, 0, tiled=True)
    input_grad, attended, gains = call(
        at_home, (shape((n, width), BF), shape((n, inner), BF), shape((HEADS, 8, d), F32)), late, w_mine, w_other,
        flops=2 * n * width * 3 * inner, scratch=[pltpu.VMEM((HEADS, n, 3 * d), BF)],
    )
    sums, _ = together(sums, gains)
    (sums,) = call(add_first, (shape((rows // 8, 3 * d), F32),), sums)
    sums = lax.all_to_all(sums, ("zh", "zm", "zl", "c"), 0, 0, tiled=True)
    gains = [gains] + [swap(gains, "dp", bit, replicas) for bit in (1, 2, 3)]
    weight_grad, gain_grad = call(
        add_up, (shape((width // 256, 3 * inner), F32), shape((HEADS, d), F32)), sums, *gains
    )
    return (attended[None], input_grad[None], weight_grad, gain_grad.reshape(inner))


def solution(mesh):
    fine = Mesh(mesh.devices.reshape(mesh.devices.shape[0], 2, 2, 2, 2, 2, 2), ALL)
    rows = P("dp", SEQ, None)
    return jax.shard_map(
        local,
        mesh=fine,
        in_specs=(rows, P("dp", None), P(), rows),
        out_specs=(rows, rows, P(ALL, None), P()),
        check_vma=False,
    )
```

```python
import jax
import jax.numpy as jnp
from jax import lax
from jax.experimental import pallas as pl
from jax.experimental.pallas import tpu as pltpu
from jax.sharding import Mesh, PartitionSpec as P

HEADS = 8
HEAD_DIM = 128
EPSILON = 1e-05
BF = jnp.bfloat16
F32 = jnp.float32

SEQ = ("yh", "yl", "zh", "zm", "zl", "c")
CUBE = ("yl", "zl", "c")
RUN = ("zh", "zm")
ALL = ("dp",) + SEQ
NN = (((1,), (0,)), ((), ()))
NT = (((1,), (1,)), ((), ()))
TN = (((0,), (0,)), ((), ()))


def swap(x, axes, bit, count):
    return lax.ppermute(x, axes, [(i, i ^ bit) for i in range(count)])


def dot(a, b, dims):
    return lax.dot_general(a, b, dims, preferred_element_type=F32)


def together(*xs):
    return lax.optimization_barrier(xs)


def call(body, outs, *operands, flops=0, scratch=(), near_in=False, near_out=False, limit=60, views=None):
    size = sum(o.size * o.dtype.itemsize for o in (*operands, *outs))
    count, total = len(operands), len(operands) + len(outs)
    moved = ([] if near_in else list(range(count))) + ([] if near_out else list(range(count, total)))
    arrays = (*operands, *outs)
    views = views or {}
    dims = [views[i][0] if i in views else x.shape for i, x in enumerate(arrays)]

    def kernel(*refs):
        given, (*copies, sems), rest = refs[:total], refs[total : total + len(moved) + 1], refs[total + len(moved) + 1 :]
        near = list(given)
        for slot, i in enumerate(moved):
            near[i] = copies[slot]
        given = [views[i][1](ref) if i in views else ref for i, ref in enumerate(given)]
        loads = {i: pltpu.make_async_copy(given[i], near[i], sems.at[i]) for i in moved if i < count}
        stores = {i - count: pltpu.make_async_copy(near[i], given[i], sems.at[i]) for i in moved if i >= count}
        waited, started = set(), set()

        def ready(*places):
            for i in places or range(count):
                if i in loads and i not in waited:
                    loads[i].wait()
                    waited.add(i)

        def finish(*places):
            for i in places or range(len(outs)):
                if i in stores and i not in started:
                    stores[i].start()
                    started.add(i)

        for load in loads.values():
            load.start()
        body(ready, finish, *near, *rest)
        ready()
        finish()
        for store in stores.values():
            store.wait()

    inside, outside = pl.BlockSpec(memory_space=pltpu.VMEM), pl.BlockSpec(memory_space=pltpu.HBM)
    return pl.pallas_call(
        kernel,
        out_shape=[o if near_out else pltpu.HBM(o.shape, o.dtype) for o in outs],
        in_specs=[inside if near_in else outside] * count,
        out_specs=[inside if near_out else outside] * len(outs),
        scratch_shapes=[pltpu.VMEM(dims[i], arrays[i].dtype) for i in moved]
        + [pltpu.SemaphoreType.DMA((total,))]
        + list(scratch),
        cost_estimate=pl.CostEstimate(flops=flops, bytes_accessed=size, transcendentals=0),
        compiler_params=pltpu.CompilerParams(vmem_limit_bytes=limit * 2**20),
    )(*operands)


def shape(dims, dtype):
    return jax.ShapeDtypeStruct(dims, dtype)


def slices(weight, tokens, grad):
    depth, d, half = weight.shape[0], HEAD_DIM, weight.shape[0] // 2
    n, width = tokens.shape

    def kernel(weight, tokens, grad, heads_out, half_out, b0, b1, b2, b3, head, half_near, tok, cols, sems):
        me, core = lax.axis_index(CUBE), lax.axis_index("c")
        loads = [(tokens, tok)]
        for k in range(4):
            at = pl.multiple_of(((me // 2) ^ k) * 2 * d, 2 * d)
            loads.append((grad.at[:, pl.ds(at, 2 * d)], cols.at[k]))
        for part in range(3):
            at = pl.multiple_of((part * HEADS + me) * d, d)
            loads.append((weight.at[:, pl.ds(at, d)], head.at[:, pl.ds(part * d, d)]))
        loads.append((weight.at[pl.ds(pl.multiple_of(core * half, half), half), :], half_near))
        loads = [pltpu.make_async_copy(x, y, sems.at[i]) for i, (x, y) in enumerate(loads)]
        stores = []
        for k, block in enumerate((b0, b1, b2, b3)):
            stores.append((tok, block.at[:, pl.ds(0, width)]))
            stores.append((cols.at[k], block.at[:, pl.ds(width, 2 * d)]))
        for j in range(4):
            stores.append((head, heads_out.at[pl.ds(j * depth, depth), :]))
        stores.append((half_near, half_out))
        stores = [pltpu.make_async_copy(x, y, sems.at[i + len(loads)]) for i, (x, y) in enumerate(stores)]
        for copy in loads:
            copy.start()
        for some, then in ((loads[:5], stores[:8]), (loads[5:8], stores[8:12]), (loads[8:], stores[12:])):
            for copy in some:
                copy.wait()
            for copy in then:
                copy.start()
        for copy in stores:
            copy.wait()

    outs = ((4 * depth, 3 * d), (half, weight.shape[1])) + ((n, width + 2 * d),) * 4
    near = ((depth, 3 * d), (half, weight.shape[1]), (n, width), (4, n, 2 * d))
    return pl.pallas_call(
        kernel,
        out_shape=[pltpu.HBM(o, BF) for o in outs],
        in_specs=[pl.BlockSpec(memory_space=pltpu.HBM)] * 3,
        out_specs=[pl.BlockSpec(memory_space=pltpu.HBM)] * len(outs),
        scratch_shapes=[pltpu.VMEM(o, BF) for o in near] + [pltpu.SemaphoreType.DMA((22,))],
        cost_estimate=pl.CostEstimate(flops=0, bytes_accessed=2**21, transcendentals=0),
        compiler_params=pltpu.CompilerParams(vmem_limit_bytes=60 * 2**20),
    )(weight, tokens, grad)


def load_rows(pieces, rows, width, sems):
    n = pieces[0].shape[0]
    me = lax.axis_index(CUBE)
    copies = []
    for k in range(8):
        place = pl.ds(pl.multiple_of((me ^ k) * n, n), n)
        copies.append(pltpu.make_async_copy(pieces[k].at[:, pl.ds(0, width)], rows.at[place, :], sems.at[k]))
        copies[-1].start()
    return copies


def project(w_cols, pieces):
    d, n = HEAD_DIM, pieces[0].shape[0]
    width, rows = w_cols.shape[0], 8 * n

    def kernel(w_far, *refs):
        pieces, (query, key, value, states, upstream, w, tokens, sems) = refs[:8], refs[8:]
        me = lax.axis_index(CUBE)
        at = pl.multiple_of(width + lax.axis_index("c") * d, d)
        first = pltpu.make_async_copy(w_far, w, sems.at[16])
        first.start()
        loads = load_rows(pieces, tokens, width, sems)
        ups = []
        for k in range(8):
            place = pl.ds(pl.multiple_of((me ^ k) * n, n), n)
            ups.append(pltpu.make_async_copy(pieces[k].at[:, pl.ds(at, d)], upstream.at[place, :], sems.at[8 + k]))
            ups[-1].start()
        first.wait()
        for p in range(4):
            loads[2 * p].wait()
            loads[2 * p + 1].wait()
            place = pl.ds(pl.multiple_of(((me // 2) ^ p) * 2 * n, 2 * n), 2 * n)
            got = dot(tokens[place, :], w[...], NN).astype(BF)
            for part, ref in enumerate((query, key, value)):
                ref[place, :] = got[:, part * d : (part + 1) * d]
        half = 4 * n
        for s in range(2):
            place = pl.ds(s * half, half)
            states[pl.ds(s * d, d), :] = dot(key[place, :], value[place, :], TN).astype(BF)
        for copy in ups:
            copy.wait()

    column = shape((rows, d), BF)
    return pl.pallas_call(
        kernel,
        out_shape=[column, column, column, shape((2 * d, d), BF), column],
        in_specs=[pl.BlockSpec(memory_space=pltpu.HBM)] * 9,
        out_specs=[pl.BlockSpec(memory_space=pltpu.VMEM)] * 5,
        scratch_shapes=[
            pltpu.VMEM(w_cols.shape, BF), pltpu.VMEM((rows, width), BF), pltpu.SemaphoreType.DMA((17,))
        ],
        cost_estimate=pl.CostEstimate(flops=2 * rows * width * 3 * d, bytes_accessed=2**22, transcendentals=0),
        compiler_params=pltpu.CompilerParams(vmem_limit_bytes=58 * 2**20),
    )(w_cols, *pieces)


def below(rows):
    return lax.broadcasted_iota(jnp.int32, (rows, rows), 0) >= lax.broadcasted_iota(jnp.int32, (rows, rows), 1)


def inside(ready, finish, query, key, value, upstream, states, scores, intra, *copies):
    for source, copy in zip((query, key, value, upstream, states), copies):
        copy[...] = source[...]
    half = query.shape[0] // 2
    keep = below(half)
    for s in range(2):
        rows = pl.ds(s * half, half)
        got = jnp.where(keep, dot(query[rows, :], key[rows, :], NT), 0.0).astype(BF)
        scores[rows, :] = got
        intra[rows, :] = dot(got, value[rows, :], NN)


def combine(ready, finish, mine, a, b, c, out):
    ready()
    d = HEAD_DIM
    total = mine[...].astype(F32) + a[...].astype(F32) + b[...].astype(F32) + c[...].astype(F32)
    out[...] = (total[:d] + total[d:]).astype(BF)


def in_parts(row):
    high = row.astype(BF).astype(F32)
    middle = (row - high).astype(BF).astype(F32)
    wide = jnp.concatenate([high, middle, row - high - middle], axis=1)
    place = lax.broadcasted_iota(jnp.int32, (16, wide.shape[1]), 0)
    return jnp.where(place == 0, wide, 0.0).astype(BF)


def states_at(mine, got, far, backward):
    d = HEAD_DIM
    place = lax.axis_index(RUN)
    total = mine[: 2 * d, :].astype(F32)
    near = jnp.zeros_like(total)
    for k, ref in enumerate(got):
        term = ref[: 2 * d, :].astype(F32)
        source = place ^ (k + 1)
        use = (source > place) if backward else (source < place)
        near = near + jnp.where(use, term, 0.0)
        total = total + term
    yh = lax.axis_index("yh")
    cross = jnp.where((yh == 0) if backward else (yh == 1), far[:d, :].astype(F32), 0.0)
    if backward:
        return near[:d] + total[d:] + cross, near[d:] + cross
    return near[:d] + cross, near[d:] + total[:d] + cross


def forward(
    ready, finish, query, intra, mine, a, b, c, far, upstream, gain, attended, mixed_grad, payload, before, gain_sum
):
    ready()
    d = HEAD_DIM
    half = query.shape[0] // 2
    scale = gain[:, pl.ds(pl.multiple_of(lax.axis_index(CUBE) * d, d), d)].astype(F32)
    gain_part = jnp.zeros((1, d), F32)
    for s, state in enumerate(states_at(mine, (a, b, c), far, False)):
        state = state.astype(BF)
        before[pl.ds(s * d, d), :] = state
        rows = pl.ds(s * half, half)
        mixed = intra[rows, :] + dot(query[rows, :], state, NN)
        inverse_rms = lax.rsqrt(jnp.mean(mixed * mixed, axis=-1, keepdims=True) + EPSILON)
        normed = mixed * inverse_rms
        attended[rows, :] = (scale * normed).astype(BF)
        up = upstream[rows, :].astype(F32)
        product = up * normed
        gain_part = gain_part + jnp.sum(product, axis=0, keepdims=True)
        along = jnp.mean(product * scale, axis=-1, keepdims=True)
        grad = (inverse_rms * (up * scale - normed * along)).astype(BF)
        mixed_grad[rows, :] = grad
        payload[pl.ds(s * d, d), :] = dot(query[rows, :], grad, TN).astype(BF)
    gain_sum[...] = jnp.broadcast_to(gain_part, gain_sum.shape)


def backward_inside(
    ready, finish, query, key, value, scores, mixed_grad, before, attended, sent, key_part, value_part
):
    ready()
    d = HEAD_DIM
    half = query.shape[0] // 2
    keep = below(half)
    for s in range(2):
        rows = pl.ds(s * half, half)
        grad = mixed_grad[rows, :]
        got = jnp.where(keep, dot(grad, value[rows, :], NT), 0.0).astype(BF)
        sent[rows, :d] = attended[rows, :]
        sent[rows, d:] = (dot(got, key[rows, :], NN) + dot(grad, before[pl.ds(s * d, d), :], NT)).astype(BF)
        key_part[rows, :] = dot(got, query[rows, :], TN)
        value_part[rows, :] = dot(scores[rows, :], grad, TN)


def backward_rest(ready, finish, key, value, sent, key_part, value_part, mine, a, b, c, far, joined, *refs):
    late, blocks = refs[:4], refs[4]
    ready()
    d = HEAD_DIM
    n = key.shape[0] // 8
    half = 4 * n
    joined[:, :d] = sent[:, d:]
    for s, state in enumerate(states_at(mine, (a, b, c), far, True)):
        state = state.astype(BF)
        rows = pl.ds(s * half, half)
        key_grad = (key_part[rows, :] + dot(value[rows, :], state, NT)).astype(BF)
        value_grad = (value_part[rows, :] + dot(key[rows, :], state, NN)).astype(BF)
        joined[rows, d : 2 * d] = key_grad
        joined[rows, 2 * d :] = value_grad
        for i in range(4):
            blocks[s * 4 + i, :, : 2 * d] = sent[pl.ds(s * half + i * n, n), :]
            blocks[s * 4 + i, :, 2 * d : 3 * d] = key_grad[i * n : (i + 1) * n]
            blocks[s * 4 + i, :, 3 * d :] = value_grad[i * n : (i + 1) * n]
    finish(0)
    chip = lax.axis_index(CUBE) // 2
    for k in range(4):
        for core in range(2):
            late[k][core] = blocks[(chip ^ k) * 2 + core]
        finish(1 + k)


def weigh(joined, gain_sum, pieces, width):
    n, d = pieces[0].shape[0], HEAD_DIM
    rows = 8 * n

    def kernel(joined_far, gain_far, *refs):
        pieces, (out_far, joined, gain, tokens, out, sems) = refs[:8], refs[8:]
        first = pltpu.make_async_copy(joined_far, joined, sems.at[8])
        second = pltpu.make_async_copy(gain_far, gain, sems.at[10])
        first.start()
        second.start()
        loads = load_rows(pieces, tokens, width, sems)
        first.wait()
        for load in loads:
            load.wait()
        second.wait()
        terms = in_parts(gain[:1, :])
        step, share = 256, width // 16
        for j in range(width // step):
            got = dot(tokens[:, j * step : (j + 1) * step].T, joined[...], NN).astype(BF)
            for i in range(step // share):
                at = (j * (step // share) + i) * (share + 16)
                out[at : at + share, :] = got[i * share : (i + 1) * share]
                out[at + share : at + share + 16, :] = terms
        last = pltpu.make_async_copy(out, out_far, sems.at[9])
        last.start()
        last.wait()

    return pl.pallas_call(
        kernel,
        out_shape=pltpu.HBM((width + 256, 3 * d), BF),
        in_specs=[pl.BlockSpec(memory_space=pltpu.HBM)] * 10,
        out_specs=pl.BlockSpec(memory_space=pltpu.HBM),
        scratch_shapes=[
            pltpu.VMEM((rows, 3 * d), BF), pltpu.VMEM((8, d), F32), pltpu.VMEM((rows, width), BF),
            pltpu.VMEM((width + 256, 3 * d), BF), pltpu.SemaphoreType.DMA((11,)),
        ],
        cost_estimate=pl.CostEstimate(flops=2 * rows * width * 3 * d, bytes_accessed=2**22, transcendentals=0),
        compiler_params=pltpu.CompilerParams(vmem_limit_bytes=60 * 2**20),
    )(joined, gain_sum, *pieces)


def at_home(ready, finish, mine, *refs):
    late, (keep, send, attended, blocks) = refs[:8], refs[8:]
    ready(*range(1, 9))
    d = HEAD_DIM
    n = attended.shape[0]
    me, core = lax.axis_index(CUBE), lax.axis_index("c")
    for k in range(HEADS):
        blocks[me ^ k, :n, :] = late[k][core]
        blocks[me ^ k, n:, :] = late[k][1 - core]
    for h in range(HEADS):
        attended[:, h * d : (h + 1) * d] = blocks[h, :n, :d]
    finish(2)
    rows = jnp.concatenate(
        [blocks[h, :, (1 + part) * d : (2 + part) * d] for part in range(3) for h in range(HEADS)], axis=1
    )
    ready(0)
    got = dot(rows, mine[...], NT).astype(BF)
    keep[...] = got[:n]
    send[...] = got[n:]


def add_first(ready, finish, pieces, out):
    ready()
    d = HEAD_DIM
    whole, width = pieces.shape[0] // 16, pieces.shape[1]
    rows = whole - 16
    for yl in range(2):
        total = sum(
            pieces[pl.ds(((dp * 2 + yh) * 2 + yl) * whole, whole), :].astype(F32) for dp in range(4) for yh in range(2)
        )
        gain = total[rows : rows + 1]
        gain = jnp.broadcast_to(gain[:, :d] + gain[:, d : 2 * d] + gain[:, 2 * d :], (4, d))
        for j in range(16):
            place = pl.ds(j * 8 + yl * 4, 4)
            out[place, :width] = total[j * 4 : j * 4 + 4, :]
            out[place, width:] = gain


def add_up(ready, finish, pieces, keep, got, weight_grad, gain_grad, input_grad):
    ready()
    d = HEAD_DIM
    for low in range(4):
        total = sum(pieces[pl.ds((run * 4 + low) * 8, 8), :] for run in range(4)) / 4
        for yl in range(2):
            h = yl * 4 + low
            for part in range(3):
                at = (part * HEADS + h) * d
                weight_grad[:, at : at + d] = total[yl * 4 : yl * 4 + 4, part * d : (part + 1) * d]
            gain_grad[h : h + 1, :] = total[yl * 4 : yl * 4 + 1, 3 * d :]
    width = keep.shape[1] // 4
    even = lax.axis_index("c") == 0
    for p in range(4):
        x, y = keep[:, p * width : (p + 1) * width], got[:, p * width : (p + 1) * width]
        input_grad[:, 2 * p * width : (2 * p + 1) * width] = jnp.where(even, x, y)
        input_grad[:, (2 * p + 1) * width : (2 * p + 2) * width] = jnp.where(even, y, x)


def local(tokens, qkv_weight, out_gain, out_grad):
    replicas = lax.axis_size("dp")
    d = HEAD_DIM
    block = tokens[0]
    n, width = block.shape
    inner = out_gain.shape[0]
    depth = qkv_weight.shape[0]

    w_heads, w_half, *blocks = slices(qkv_weight, block, out_grad[0])
    near = [swap(blocks[bit], ("yl", "zl"), bit, 4) for bit in (1, 2, 3)]
    w_cols = lax.all_to_all(w_heads, "dp", 0, 0, tiled=True)
    mine, _ = together(blocks[0], near[0])
    pieces = [x for side in [mine] + near for x in (side, swap(side, "c", 1, 2))]

    rows = 8 * n
    column, square = shape((rows, d), BF), shape((2 * d, d), BF)
    query, key, value, states, upstream = project(w_cols, pieces)
    w_half, _ = together(w_half, states)
    w_mine = lax.all_gather(w_half, "dp", axis=0, tiled=True)
    got = [swap(states, RUN, bit, 4) for bit in (1, 2, 3)]
    scores, intra, query, key, value, upstream, states = call(
        inside, (shape((rows, rows // 2), BF), shape((rows, d), F32), column, column, column, column, square),
        query, key, value, upstream, states, flops=2 * rows * rows * d, near_in=True, near_out=True, limit=12,
    )
    scores, *got = together(scores, *got)
    (both,) = call(combine, (shape((d, d), BF),), states, *got, near_in=True, near_out=True, limit=12)
    far = swap(both, "yh", 1, 2)
    attended_head, mixed_grad, payload, before, gain_sum = call(
        forward, (column, column, square, square, shape((8, d), F32)),
        query, intra, states, *got, far, upstream, out_gain.reshape(1, inner), flops=4 * rows * d * d, near_in=True, near_out=True, limit=12,
    )
    grads = [swap(payload, RUN, bit, 4) for bit in (1, 2, 3)]
    (both_grad,) = call(combine, (shape((d, d), BF),), payload, *grads, near_in=True, near_out=True, limit=12)
    mixed_grad, both_grad = together(mixed_grad, both_grad)
    sent, key_part, value_part = call(
        backward_inside, (shape((rows, 2 * d), BF), shape((rows, d), F32), shape((rows, d), F32)),
        query, key, value, scores, mixed_grad, before, attended_head, flops=4 * rows * rows * d, near_in=True, near_out=True, limit=12,
    )
    far_grad = swap(both_grad, "yh", 1, 2)
    joined, *late = call(
        backward_rest, (shape((rows, 3 * d), BF),) + (shape((2, n, 4 * d), BF),) * 4,
        key, value, sent, key_part, value_part, payload, *grads, far_grad, flops=8 * rows * d * d,
        near_in=True, limit=16, scratch=[pltpu.VMEM((HEADS, n, 4 * d), BF)],
    )
    late = [late[0]] + [swap(late[bit], ("yl", "zl"), bit, 4) for bit in (1, 2, 3)]
    weight_part = weigh(joined, gain_sum, pieces, width)
    sums = lax.all_to_all(weight_part, ("dp", "yh", "yl"), 0, 0, tiled=True)
    (sums,) = call(add_first, (shape((rows // 8, 4 * d), F32),), sums)
    *late, _ = together(*late, sums)
    late = [x for side in late for x in (side, swap(side, "c", 1, 2))]
    sums = lax.all_to_all(sums, ("zh", "zm", "zl", "c"), 0, 0, tiled=True)
    half = shape((n, width // 2), BF)
    keep, send, attended = call(
        at_home, (half, half, shape((n, inner), BF)), w_mine, *late,
        flops=2 * n * width * 3 * inner, scratch=[pltpu.VMEM((HEADS, 2 * n, 4 * d), BF)],
    )
    got = swap(send, "c", 1, 2)
    sums, got = together(sums, got)
    weight_grad, gain_grad, input_grad = call(
        add_up, (shape((width // 256, 3 * inner), F32), shape((HEADS, d), F32), shape((n, width), BF)), sums, keep, got
    )
    return (attended[None], input_grad[None], weight_grad, gain_grad.reshape(inner))


def solution(mesh):
    fine = Mesh(mesh.devices.reshape(mesh.devices.shape[0], 2, 2, 2, 2, 2, 2), ALL)
    rows = P("dp", SEQ, None)
    return jax.shard_map(
        local,
        mesh=fine,
        in_specs=(rows, P("dp", None), P(), rows),
        out_specs=(rows, rows, P(ALL, None), P()),
        check_vma=False,
    )
```

```python
import jax
import jax.numpy as jnp
from jax import lax
from jax.experimental import pallas as pl
from jax.experimental.pallas import tpu as pltpu
from jax.sharding import Mesh, PartitionSpec as P

HEADS = 8
HEAD_DIM = 128
EPSILON = 1e-05
BF = jnp.bfloat16
F32 = jnp.float32

SEQ = ("yh", "yl", "zh", "zm", "zl", "c")
CUBE = ("yl", "zl", "c")
RUN = ("zh", "zm")
ALL = ("dp",) + SEQ
NN = (((1,), (0,)), ((), ()))
NT = (((1,), (1,)), ((), ()))
TN = (((0,), (0,)), ((), ()))


def swap(x, axes, bit, count):
    return lax.ppermute(x, axes, [(i, i ^ bit) for i in range(count)])


def dot(a, b, dims):
    return lax.dot_general(a, b, dims, preferred_element_type=F32)


def together(*xs):
    return lax.optimization_barrier(xs)


def call(body, outs, *operands, flops=0, scratch=(), near_in=False, near_out=False, limit=60, views=None):
    size = sum(o.size * o.dtype.itemsize for o in (*operands, *outs))
    count, total = len(operands), len(operands) + len(outs)
    moved = ([] if near_in else list(range(count))) + ([] if near_out else list(range(count, total)))
    arrays = (*operands, *outs)
    views = views or {}
    dims = [views[i][0] if i in views else x.shape for i, x in enumerate(arrays)]

    def kernel(*refs):
        given, copies, rest = refs[:total], refs[total : total + len(moved)], refs[total + len(moved) :]
        sems, rest = (rest[0], rest[1:]) if moved else (None, rest)
        slots = {i: slot for slot, i in enumerate(moved)}
        near = list(given)
        for slot, i in enumerate(moved):
            near[i] = copies[slot]
        given = [views[i][1](ref) if i in views else ref for i, ref in enumerate(given)]
        loads = {i: pltpu.make_async_copy(given[i], near[i], sems.at[slots[i]]) for i in moved if i < count}
        stores = {i - count: pltpu.make_async_copy(near[i], given[i], sems.at[slots[i]]) for i in moved if i >= count}
        waited, started = set(), set()

        def ready(*places):
            for i in places or range(count):
                if i in loads and i not in waited:
                    loads[i].wait()
                    waited.add(i)

        def finish(*places):
            for i in places or range(len(outs)):
                if i in stores and i not in started:
                    stores[i].start()
                    started.add(i)

        for load in loads.values():
            load.start()
        body(ready, finish, *near, *rest)
        ready()
        finish()
        for store in stores.values():
            store.wait()

    inside, outside = pl.BlockSpec(memory_space=pltpu.VMEM), pl.BlockSpec(memory_space=pltpu.HBM)
    return pl.pallas_call(
        kernel,
        out_shape=[o if near_out else pltpu.HBM(o.shape, o.dtype) for o in outs],
        in_specs=[inside if near_in else outside] * count,
        out_specs=[inside if near_out else outside] * len(outs),
        scratch_shapes=[pltpu.VMEM(dims[i], arrays[i].dtype) for i in moved]
        + ([pltpu.SemaphoreType.DMA((len(moved),))] if moved else [])
        + list(scratch),
        cost_estimate=pl.CostEstimate(flops=flops, bytes_accessed=size, transcendentals=0),
        compiler_params=pltpu.CompilerParams(vmem_limit_bytes=limit * 2**20),
    )(*operands)


def shape(dims, dtype):
    return jax.ShapeDtypeStruct(dims, dtype)


def slices(weight, tokens, grad):
    depth, d = weight.shape[0], HEAD_DIM
    n, width = tokens.shape

    def kernel(weight, tokens, grad, heads_out, b0, b1, b2, b3, head, tok, cols, sems):
        me = lax.axis_index(CUBE)
        loads = [(tokens, tok)]
        for k in range(4):
            at = pl.multiple_of(((me // 2) ^ k) * 2 * d, 2 * d)
            loads.append((grad.at[:, pl.ds(at, 2 * d)], cols.at[k]))
        for part in range(3):
            at = pl.multiple_of((part * HEADS + me) * d, d)
            loads.append((weight.at[:, pl.ds(at, d)], head.at[:, pl.ds(part * d, d)]))
        loads = [pltpu.make_async_copy(x, y, sems.at[i]) for i, (x, y) in enumerate(loads)]
        stores = []
        for k, block in enumerate((b0, b1, b2, b3)):
            stores.append((tok, block.at[:, pl.ds(0, width)]))
            stores.append((cols.at[k], block.at[:, pl.ds(width, 2 * d)]))
        for j in range(4):
            stores.append((head, heads_out.at[pl.ds(j * depth, depth), :]))
        stores = [pltpu.make_async_copy(x, y, sems.at[i + len(loads)]) for i, (x, y) in enumerate(stores)]
        for copy in loads:
            copy.start()
        for some, then in ((loads[:5], stores[:8]), (loads[5:], stores[8:])):
            for copy in some:
                copy.wait()
            for copy in then:
                copy.start()
        for copy in stores:
            copy.wait()

    outs = ((4 * depth, 3 * d),) + ((n, width + 2 * d),) * 4
    near = ((depth, 3 * d), (n, width), (4, n, 2 * d))
    return pl.pallas_call(
        kernel,
        out_shape=[pltpu.HBM(o, BF) for o in outs],
        in_specs=[pl.BlockSpec(memory_space=pltpu.HBM)] * 3,
        out_specs=[pl.BlockSpec(memory_space=pltpu.HBM)] * len(outs),
        scratch_shapes=[pltpu.VMEM(o, BF) for o in near] + [pltpu.SemaphoreType.DMA((20,))],
        cost_estimate=pl.CostEstimate(flops=0, bytes_accessed=2**21, transcendentals=0),
        compiler_params=pltpu.CompilerParams(vmem_limit_bytes=60 * 2**20),
    )(weight, tokens, grad)


def half_rows(weight):
    half = weight.shape[0] // 2

    def kernel(weight, out, near, sems):
        at = pl.multiple_of(lax.axis_index("c") * half, half)
        load = pltpu.make_async_copy(weight.at[pl.ds(at, half), :], near, sems.at[0])
        load.start()
        load.wait()
        store = pltpu.make_async_copy(near, out, sems.at[1])
        store.start()
        store.wait()

    return pl.pallas_call(
        kernel,
        out_shape=pltpu.HBM((half, weight.shape[1]), BF),
        in_specs=[pl.BlockSpec(memory_space=pltpu.HBM)],
        out_specs=pl.BlockSpec(memory_space=pltpu.HBM),
        scratch_shapes=[pltpu.VMEM((half, weight.shape[1]), BF), pltpu.SemaphoreType.DMA((2,))],
        cost_estimate=pl.CostEstimate(flops=0, bytes_accessed=2**21, transcendentals=0),
        compiler_params=pltpu.CompilerParams(vmem_limit_bytes=60 * 2**20),
    )(weight)


def load_rows(pieces, rows, width, sems):
    n = pieces[0].shape[0]
    me = lax.axis_index(CUBE)
    copies = []
    for k in range(8):
        place = pl.ds(pl.multiple_of((me ^ k) * n, n), n)
        copies.append(pltpu.make_async_copy(pieces[k].at[:, pl.ds(0, width)], rows.at[place, :], sems.at[k]))
        copies[-1].start()
    return copies


def project(w_cols, pieces):
    d, n = HEAD_DIM, pieces[0].shape[0]
    width, rows = w_cols.shape[0], 8 * n

    def kernel(w_far, *refs):
        pieces, (query, key, value, states, upstream, w, tokens, sems) = refs[:8], refs[8:]
        at = pl.multiple_of(width + lax.axis_index("c") * d, d)
        me = lax.axis_index(CUBE)
        first = pltpu.make_async_copy(w_far, w, sems.at[16])
        first.start()
        loads = load_rows(pieces, tokens, width, sems)
        ups = []
        for k in range(8):
            place = pl.ds(pl.multiple_of((me ^ k) * n, n), n)
            ups.append(pltpu.make_async_copy(pieces[k].at[:, pl.ds(at, d)], upstream.at[place, :], sems.at[8 + k]))
            ups[-1].start()
        first.wait()
        for load in loads:
            load.wait()
        got = dot(tokens[...], w[...], NN).astype(BF)
        for part, ref in enumerate((query, key, value)):
            ref[...] = got[:, part * d : (part + 1) * d]
        half = 4 * n
        for s in range(2):
            place = pl.ds(s * half, half)
            states[pl.ds(s * d, d), :] = dot(key[place, :], value[place, :], TN).astype(BF)
        for copy in ups:
            copy.wait()

    column = shape((rows, d), BF)
    return pl.pallas_call(
        kernel,
        out_shape=[column, column, column, shape((2 * d, d), BF), column],
        in_specs=[pl.BlockSpec(memory_space=pltpu.HBM)] * 9,
        out_specs=[pl.BlockSpec(memory_space=pltpu.VMEM)] * 5,
        scratch_shapes=[
            pltpu.VMEM(w_cols.shape, BF), pltpu.VMEM((rows, width), BF), pltpu.SemaphoreType.DMA((17,))
        ],
        cost_estimate=pl.CostEstimate(flops=2 * rows * width * 3 * d, bytes_accessed=2**22, transcendentals=0),
        compiler_params=pltpu.CompilerParams(vmem_limit_bytes=58 * 2**20),
    )(w_cols, *pieces)


def below(rows):
    return lax.broadcasted_iota(jnp.int32, (rows, rows), 0) >= lax.broadcasted_iota(jnp.int32, (rows, rows), 1)


def inside(ready, finish, query, key, value, upstream, states, scores, intra, *copies):
    for source, copy in zip((query, key, value, upstream, states), copies):
        copy[...] = source[...]
    half = query.shape[0] // 2
    keep = below(half)
    for s in range(2):
        rows = pl.ds(s * half, half)
        got = jnp.where(keep, dot(query[rows, :], key[rows, :], NT), 0.0).astype(BF)
        scores[rows, :] = got
        intra[rows, :] = dot(got, value[rows, :], NN)


def combine(ready, finish, mine, a, b, c, out):
    ready()
    d = HEAD_DIM
    total = mine[...].astype(F32) + a[...].astype(F32) + b[...].astype(F32) + c[...].astype(F32)
    out[...] = (total[:d] + total[d:]).astype(BF)


def in_parts(row):
    high = row.astype(BF).astype(F32)
    middle = (row - high).astype(BF).astype(F32)
    wide = jnp.concatenate([high, middle, row - high - middle], axis=1)
    place = lax.broadcasted_iota(jnp.int32, (16, wide.shape[1]), 0)
    return jnp.where(place == 0, wide, 0.0).astype(BF)


def states_at(mine, got, far, backward):
    d = HEAD_DIM
    place = lax.axis_index(RUN)
    total = mine[: 2 * d, :].astype(F32)
    near = jnp.zeros_like(total)
    for k, ref in enumerate(got):
        term = ref[: 2 * d, :].astype(F32)
        source = place ^ (k + 1)
        use = (source > place) if backward else (source < place)
        near = near + jnp.where(use, term, 0.0)
        total = total + term
    yh = lax.axis_index("yh")
    cross = jnp.where((yh == 0) if backward else (yh == 1), far[:d, :].astype(F32), 0.0)
    if backward:
        return near[:d] + total[d:] + cross, near[d:] + cross
    return near[:d] + cross, near[d:] + total[:d] + cross


def forward(
    ready, finish, query, intra, mine, a, b, c, far, upstream, gain, attended, mixed_grad, payload, before, gain_sum
):
    ready()
    d = HEAD_DIM
    half = query.shape[0] // 2
    scale = gain[:, pl.ds(pl.multiple_of(lax.axis_index(CUBE) * d, d), d)].astype(F32)
    gain_part = jnp.zeros((1, d), F32)
    for s, state in enumerate(states_at(mine, (a, b, c), far, False)):
        state = state.astype(BF)
        before[pl.ds(s * d, d), :] = state
        rows = pl.ds(s * half, half)
        mixed = intra[rows, :] + dot(query[rows, :], state, NN)
        inverse_rms = lax.rsqrt(jnp.mean(mixed * mixed, axis=-1, keepdims=True) + EPSILON)
        normed = mixed * inverse_rms
        attended[rows, :] = (scale * normed).astype(BF)
        up = upstream[rows, :].astype(F32)
        product = up * normed
        gain_part = gain_part + jnp.sum(product, axis=0, keepdims=True)
        along = jnp.mean(product * scale, axis=-1, keepdims=True)
        grad = (inverse_rms * (up * scale - normed * along)).astype(BF)
        mixed_grad[rows, :] = grad
        payload[pl.ds(s * d, d), :] = dot(query[rows, :], grad, TN).astype(BF)
    gain_sum[...] = jnp.broadcast_to(gain_part, gain_sum.shape)


def backward_inside(
    ready, finish, query, key, value, scores, mixed_grad, before, attended, sent, key_part, value_part
):
    ready()
    d = HEAD_DIM
    half = query.shape[0] // 2
    keep = below(half)
    for s in range(2):
        rows = pl.ds(s * half, half)
        grad = mixed_grad[rows, :]
        got = jnp.where(keep, dot(grad, value[rows, :], NT), 0.0).astype(BF)
        sent[rows, :d] = attended[rows, :]
        sent[rows, d:] = (dot(got, key[rows, :], NN) + dot(grad, before[pl.ds(s * d, d), :], NT)).astype(BF)
        key_part[rows, :] = dot(got, query[rows, :], TN)
        value_part[rows, :] = dot(scores[rows, :], grad, TN)


def backward_rest(ready, finish, key, value, sent, key_part, value_part, mine, a, b, c, far, joined, *refs):
    late, blocks = refs[:4], refs[4]
    ready()
    d = HEAD_DIM
    n = key.shape[0] // 8
    half = 4 * n
    joined[:, :d] = sent[:, d:]
    for s, state in enumerate(states_at(mine, (a, b, c), far, True)):
        state = state.astype(BF)
        rows = pl.ds(s * half, half)
        key_grad = (key_part[rows, :] + dot(value[rows, :], state, NT)).astype(BF)
        value_grad = (value_part[rows, :] + dot(key[rows, :], state, NN)).astype(BF)
        joined[rows, d : 2 * d] = key_grad
        joined[rows, 2 * d :] = value_grad
        for i in range(4):
            blocks[s * 4 + i, :, : 2 * d] = sent[pl.ds(s * half + i * n, n), :]
            blocks[s * 4 + i, :, 2 * d : 3 * d] = key_grad[i * n : (i + 1) * n]
            blocks[s * 4 + i, :, 3 * d :] = value_grad[i * n : (i + 1) * n]
    finish(0)
    chip = lax.axis_index(CUBE) // 2
    for k in range(4):
        for core in range(2):
            late[k][core] = blocks[(chip ^ k) * 2 + core]
        finish(1 + k)


def weigh(joined, gain_sum, pieces, width):
    n, d = pieces[0].shape[0], HEAD_DIM
    rows = 8 * n

    def kernel(joined_far, gain_far, *refs):
        pieces, (out_far, joined, gain, tokens, out, sems) = refs[:8], refs[8:]
        first = pltpu.make_async_copy(joined_far, joined, sems.at[8])
        second = pltpu.make_async_copy(gain_far, gain, sems.at[10])
        first.start()
        second.start()
        loads = load_rows(pieces, tokens, width, sems)
        first.wait()
        for load in loads:
            load.wait()
        second.wait()
        terms = in_parts(gain[:1, :])
        step, share = 256, width // 4
        for j in range(width // step):
            got = dot(tokens[:, j * step : (j + 1) * step].T, joined[...], NN).astype(BF)
            for i in range(step // share):
                at = (j * (step // share) + i) * (share + 16)
                out[at : at + share, :] = got[i * share : (i + 1) * share]
                out[at + share : at + share + 16, :] = terms
        last = pltpu.make_async_copy(out, out_far, sems.at[9])
        last.start()
        last.wait()

    return pl.pallas_call(
        kernel,
        out_shape=pltpu.HBM((width + 64, 3 * d), BF),
        in_specs=[pl.BlockSpec(memory_space=pltpu.HBM)] * 10,
        out_specs=pl.BlockSpec(memory_space=pltpu.HBM),
        scratch_shapes=[
            pltpu.VMEM((rows, 3 * d), BF), pltpu.VMEM((8, d), F32), pltpu.VMEM((rows, width), BF),
            pltpu.VMEM((width + 64, 3 * d), BF), pltpu.SemaphoreType.DMA((11,)),
        ],
        cost_estimate=pl.CostEstimate(flops=2 * rows * width * 3 * d, bytes_accessed=2**22, transcendentals=0),
        compiler_params=pltpu.CompilerParams(vmem_limit_bytes=60 * 2**20),
    )(joined, gain_sum, *pieces)


def at_home(ready, finish, mine, *refs):
    late, (keep, send, attended, blocks) = refs[:8], refs[8:]
    ready(*range(1, 9))
    d = HEAD_DIM
    n = attended.shape[0]
    me, core = lax.axis_index(CUBE), lax.axis_index("c")
    for k in range(HEADS):
        blocks[me ^ k, :n, :] = late[k][core]
        blocks[me ^ k, n:, :] = late[k][1 - core]
    for h in range(HEADS):
        attended[:, h * d : (h + 1) * d] = blocks[h, :n, :d]
    finish(2)
    rows = jnp.concatenate(
        [blocks[h, :, (1 + part) * d : (2 + part) * d] for part in range(3) for h in range(HEADS)], axis=1
    )
    ready(0)
    got = dot(rows, mine[...], NT).astype(BF)
    keep[...] = got[:n]
    send[...] = got[n:]


def add_first(ready, finish, pieces, out):
    ready()
    d = HEAD_DIM
    whole = pieces.shape[0] // 4
    rows = whole - 16
    total = sum(pieces[pl.ds(dp * whole, whole), :].astype(F32) for dp in range(4))
    gain = total[rows : rows + 1]
    gain = in_parts(gain[:, :d] + gain[:, d : 2 * d] + gain[:, 2 * d :])[:1, :].astype(F32)
    place = lax.broadcasted_iota(jnp.int32, (4, d), 0)
    parts = jnp.where(place == 0, gain[:, :d], jnp.where(place == 1, gain[:, d : 2 * d], gain[:, 2 * d :]))
    parts = jnp.where(place == 3, 0.0, parts)
    for j in range(rows // 4):
        four = total[j * 4 : j * 4 + 4]
        message = jnp.concatenate([four[:, :d], four[:, d : 2 * d], four[:, 2 * d :], parts], axis=0)
        out[j * 16 : j * 16 + 16, :] = message.astype(BF)


def add_up(ready, finish, pieces, keep, got, weight_grad, gain_grad, input_grad):
    ready()
    d = HEAD_DIM
    for h in range(HEADS):
        yl, low = h // 4, h % 4
        places = [((yh * 2 + yl) * 4 + run) * 4 + low for yh in range(2) for run in range(4)]
        total = sum(pieces[i * 16 : i * 16 + 16, :].astype(F32) for i in places) / 4
        for part in range(3):
            at = (part * HEADS + h) * d
            weight_grad[:, at : at + d] = total[part * 4 : part * 4 + 4]
        gain_grad[h : h + 1, :] = jnp.sum(total[12:], axis=0, keepdims=True)
    width = keep.shape[1] // 4
    even = lax.axis_index("c") == 0
    for p in range(4):
        x, y = keep[:, p * width : (p + 1) * width], got[:, p * width : (p + 1) * width]
        input_grad[:, 2 * p * width : (2 * p + 1) * width] = jnp.where(even, x, y)
        input_grad[:, (2 * p + 1) * width : (2 * p + 2) * width] = jnp.where(even, y, x)


def local(tokens, qkv_weight, out_gain, out_grad):
    replicas = lax.axis_size("dp")
    d = HEAD_DIM
    block = tokens[0]
    n, width = block.shape
    inner = out_gain.shape[0]
    depth = qkv_weight.shape[0]

    w_heads, *blocks = slices(qkv_weight, block, out_grad[0])
    near = [swap(blocks[bit], ("yl", "zl"), bit, 4) for bit in (1, 2, 3)]
    w_cols = lax.all_to_all(w_heads, "dp", 0, 0, tiled=True)
    w_half = half_rows(qkv_weight)
    mine, *_ = together(blocks[0], near[0], w_half)
    pieces = [x for side in [mine] + near for x in (side, swap(side, "c", 1, 2))]

    rows = 8 * n
    column, square = shape((rows, d), BF), shape((2 * d, d), BF)
    query, key, value, states, upstream = project(w_cols, pieces)
    w_half, _ = together(w_half, states)
    w_mine = lax.all_gather(w_half, "dp", axis=0, tiled=True)
    got = [swap(states, RUN, bit, 4) for bit in (1, 2, 3)]
    scores, intra, query, key, value, upstream, states = call(
        inside, (shape((rows, rows // 2), BF), shape((rows, d), F32), column, column, column, column, square),
        query, key, value, upstream, states, flops=2 * rows * rows * d, near_in=True, near_out=True, limit=12,
    )
    scores, *got = together(scores, *got)
    (both,) = call(combine, (shape((d, d), BF),), states, *got, near_in=True, near_out=True, limit=12)
    far = swap(both, "yh", 1, 2)
    attended_head, mixed_grad, payload, before, gain_sum = call(
        forward, (column, column, square, square, shape((8, d), F32)),
        query, intra, states, *got, far, upstream, out_gain.reshape(1, inner), flops=4 * rows * d * d, near_in=True, near_out=True, limit=12,
    )
    grads = [swap(payload, RUN, bit, 4) for bit in (1, 2, 3)]
    (both_grad,) = call(combine, (shape((d, d), BF),), payload, *grads, near_in=True, near_out=True, limit=12)
    mixed_grad, both_grad = together(mixed_grad, both_grad)
    sent, key_part, value_part = call(
        backward_inside, (shape((rows, 2 * d), BF), shape((rows, d), F32), shape((rows, d), F32)),
        query, key, value, scores, mixed_grad, before, attended_head, flops=4 * rows * rows * d, near_in=True, near_out=True, limit=12,
    )
    far_grad = swap(both_grad, "yh", 1, 2)
    joined, *late = call(
        backward_rest, (shape((rows, 3 * d), BF),) + (shape((2, n, 4 * d), BF),) * 4,
        key, value, sent, key_part, value_part, payload, *grads, far_grad, flops=8 * rows * d * d,
        near_in=True, limit=16, scratch=[pltpu.VMEM((HEADS, n, 4 * d), BF)],
    )
    late = [late[0]] + [swap(late[bit], ("yl", "zl"), bit, 4) for bit in (1, 2, 3)]
    weight_part = weigh(joined, gain_sum, pieces, width)
    sums = lax.all_to_all(weight_part, "dp", 0, 0, tiled=True)
    (sums,) = call(add_first, (shape((width, d), BF),), sums, near_in=True, limit=12)
    *late, _ = together(*late, sums)
    late = [x for side in late for x in (side, swap(side, "c", 1, 2))]
    sums = lax.all_to_all(sums, SEQ, 0, 0, tiled=True)
    half = shape((n, width // 2), BF)
    keep, send, attended = call(
        at_home, (half, half, shape((n, inner), BF)), w_mine, *late,
        flops=2 * n * width * 3 * inner, scratch=[pltpu.VMEM((HEADS, 2 * n, 4 * d), BF)],
    )
    got = swap(send, "c", 1, 2)
    sums, got = together(sums, got)
    weight_grad, gain_grad, input_grad = call(
        add_up, (shape((width // 256, 3 * inner), F32), shape((HEADS, d), F32), shape((n, width), BF)), sums, keep, got,
        near_in=True, limit=12,
    )
    return (attended[None], input_grad[None], weight_grad, gain_grad.reshape(inner))


def solution(mesh):
    fine = Mesh(mesh.devices.reshape(mesh.devices.shape[0], 2, 2, 2, 2, 2, 2), ALL)
    rows = P("dp", SEQ, None)
    return jax.shard_map(
        local,
        mesh=fine,
        in_specs=(rows, P("dp", None), P(), rows),
        out_specs=(rows, rows, P(ALL, None), P()),
        check_vma=False,
    )
```

```python
import jax
import jax.numpy as jnp
from jax import lax
from jax.experimental import pallas as pl
from jax.experimental.pallas import tpu as pltpu
from jax.sharding import Mesh, PartitionSpec as P

HEADS = 8
HEAD_DIM = 128
EPSILON = 1e-05
BF = jnp.bfloat16
F32 = jnp.float32

SEQ = ("yh", "yl", "zh", "zm", "zl", "c")
CUBE = ("yl", "zl", "c")
RUN = ("zh", "zm")
ALL = ("dp",) + SEQ
NN = (((1,), (0,)), ((), ()))
NT = (((1,), (1,)), ((), ()))
TN = (((0,), (0,)), ((), ()))


def swap(x, axes, bit, count):
    return lax.ppermute(x, axes, [(i, i ^ bit) for i in range(count)])


def dot(a, b, dims):
    return lax.dot_general(a, b, dims, preferred_element_type=F32)


def together(*xs):
    return lax.optimization_barrier(xs)


def call(body, outs, *operands, flops=0, scratch=(), near_in=False, near_out=False, limit=60, views=None):
    size = sum(o.size * o.dtype.itemsize for o in (*operands, *outs))
    count, total = len(operands), len(operands) + len(outs)
    moved = ([] if near_in else list(range(count))) + ([] if near_out else list(range(count, total)))
    arrays = (*operands, *outs)
    views = views or {}
    dims = [views[i][0] if i in views else x.shape for i, x in enumerate(arrays)]

    def kernel(*refs):
        given, copies, rest = refs[:total], refs[total : total + len(moved)], refs[total + len(moved) :]
        sems, rest = (rest[0], rest[1:]) if moved else (None, rest)
        slots = {i: slot for slot, i in enumerate(moved)}
        near = list(given)
        for slot, i in enumerate(moved):
            near[i] = copies[slot]
        given = [views[i][1](ref) if i in views else ref for i, ref in enumerate(given)]
        loads = {i: pltpu.make_async_copy(given[i], near[i], sems.at[slots[i]]) for i in moved if i < count}
        stores = {i - count: pltpu.make_async_copy(near[i], given[i], sems.at[slots[i]]) for i in moved if i >= count}
        waited, started = set(), set()

        def ready(*places):
            for i in places or range(count):
                if i in loads and i not in waited:
                    loads[i].wait()
                    waited.add(i)

        def finish(*places):
            for i in places or range(len(outs)):
                if i in stores and i not in started:
                    stores[i].start()
                    started.add(i)

        for load in loads.values():
            load.start()
        body(ready, finish, *near, *rest)
        ready()
        finish()
        for store in stores.values():
            store.wait()

    inside, outside = pl.BlockSpec(memory_space=pltpu.VMEM), pl.BlockSpec(memory_space=pltpu.HBM)
    return pl.pallas_call(
        kernel,
        out_shape=[o if near_out else pltpu.HBM(o.shape, o.dtype) for o in outs],
        in_specs=[inside if near_in else outside] * count,
        out_specs=[inside if near_out else outside] * len(outs),
        scratch_shapes=[pltpu.VMEM(dims[i], arrays[i].dtype) for i in moved]
        + ([pltpu.SemaphoreType.DMA((len(moved),))] if moved else [])
        + list(scratch),
        cost_estimate=pl.CostEstimate(flops=flops, bytes_accessed=size, transcendentals=0),
        compiler_params=pltpu.CompilerParams(vmem_limit_bytes=limit * 2**20),
    )(*operands)


def shape(dims, dtype):
    return jax.ShapeDtypeStruct(dims, dtype)


def slices(weight, tokens, grad):
    depth, d = weight.shape[0], HEAD_DIM
    n, width = tokens.shape

    def kernel(weight, tokens, grad, heads_out, b0, b1, b2, b3, head, tok, cols, sems):
        me = lax.axis_index(CUBE)
        loads = [(tokens, tok)]
        for k in range(4):
            at = pl.multiple_of(((me // 2) ^ k) * 2 * d, 2 * d)
            loads.append((grad.at[:, pl.ds(at, 2 * d)], cols.at[k]))
        for part in range(3):
            at = pl.multiple_of((part * HEADS + me) * d, d)
            loads.append((weight.at[:, pl.ds(at, d)], head.at[:, pl.ds(part * d, d)]))
        loads = [pltpu.make_async_copy(x, y, sems.at[i]) for i, (x, y) in enumerate(loads)]
        stores = []
        for k, block in enumerate((b0, b1, b2, b3)):
            stores.append((tok, block.at[:, pl.ds(0, width)]))
            stores.append((cols.at[k], block.at[:, pl.ds(width, 2 * d)]))
        for j in range(4):
            stores.append((head, heads_out.at[pl.ds(j * depth, depth), :]))
        stores = [pltpu.make_async_copy(x, y, sems.at[i + len(loads)]) for i, (x, y) in enumerate(stores)]
        for copy in loads:
            copy.start()
        for some, then in ((loads[:5], stores[:8]), (loads[5:], stores[8:])):
            for copy in some:
                copy.wait()
            for copy in then:
                copy.start()
        for copy in stores:
            copy.wait()

    outs = ((4 * depth, 3 * d),) + ((n, width + 2 * d),) * 4
    near = ((depth, 3 * d), (n, width), (4, n, 2 * d))
    return pl.pallas_call(
        kernel,
        out_shape=[pltpu.HBM(o, BF) for o in outs],
        in_specs=[pl.BlockSpec(memory_space=pltpu.HBM)] * 3,
        out_specs=[pl.BlockSpec(memory_space=pltpu.HBM)] * len(outs),
        scratch_shapes=[pltpu.VMEM(o, BF) for o in near] + [pltpu.SemaphoreType.DMA((20,))],
        cost_estimate=pl.CostEstimate(flops=0, bytes_accessed=2**21, transcendentals=0),
        compiler_params=pltpu.CompilerParams(vmem_limit_bytes=60 * 2**20),
    )(weight, tokens, grad)


def half_rows(weight):
    half = weight.shape[0] // 2

    def kernel(weight, out, near, sems):
        at = pl.multiple_of(lax.axis_index("c") * half, half)
        load = pltpu.make_async_copy(weight.at[pl.ds(at, half), :], near, sems.at[0])
        load.start()
        load.wait()
        store = pltpu.make_async_copy(near, out, sems.at[1])
        store.start()
        store.wait()

    return pl.pallas_call(
        kernel,
        out_shape=pltpu.HBM((half, weight.shape[1]), BF),
        in_specs=[pl.BlockSpec(memory_space=pltpu.HBM)],
        out_specs=pl.BlockSpec(memory_space=pltpu.HBM),
        scratch_shapes=[pltpu.VMEM((half, weight.shape[1]), BF), pltpu.SemaphoreType.DMA((2,))],
        cost_estimate=pl.CostEstimate(flops=0, bytes_accessed=2**21, transcendentals=0),
        compiler_params=pltpu.CompilerParams(vmem_limit_bytes=60 * 2**20),
    )(weight)


def load_rows(pieces, rows, sems):
    n = pieces[0].shape[0]
    me = lax.axis_index(CUBE)
    copies = []
    for k in range(8):
        place = pl.ds(pl.multiple_of((me ^ k) * n, n), n)
        copies.append(pltpu.make_async_copy(pieces[k], rows.at[place, :], sems.at[k]))
        copies[-1].start()
    return copies


def project(w_cols, pieces):
    d, n = HEAD_DIM, pieces[0].shape[0]
    width, rows = w_cols.shape[0], 8 * n

    def kernel(w_far, *refs):
        pieces, (packed, states, w, tokens, sems) = refs[:8], refs[8:]
        at = pl.multiple_of(width + lax.axis_index("c") * d, d)
        first = pltpu.make_async_copy(w_far, w, sems.at[8])
        first.start()
        loads = load_rows(pieces, tokens, sems)
        first.wait()
        for load in loads:
            load.wait()
        packed[3 * rows : 4 * rows, :] = tokens[:, pl.ds(at, d)]
        got = dot(tokens[:, :width], w[...], NN).astype(BF)
        for part in range(3):
            packed[part * rows : (part + 1) * rows, :] = got[:, part * d : (part + 1) * d]
        half = 4 * n
        for s in range(2):
            key, value = packed[pl.ds(rows + s * half, half), :], packed[pl.ds(2 * rows + s * half, half), :]
            states[pl.ds(s * d, d), :] = dot(key, value, TN).astype(BF)
        packed[4 * rows :, :] = states[...]

    return pl.pallas_call(
        kernel,
        out_shape=[shape((4 * rows + 2 * d, d), BF), shape((2 * d, d), BF)],
        in_specs=[pl.BlockSpec(memory_space=pltpu.HBM)] * 9,
        out_specs=[pl.BlockSpec(memory_space=pltpu.VMEM)] * 2,
        scratch_shapes=[
            pltpu.VMEM(w_cols.shape, BF), pltpu.VMEM((rows, pieces[0].shape[1]), BF), pltpu.SemaphoreType.DMA((9,))
        ],
        cost_estimate=pl.CostEstimate(flops=2 * rows * width * 3 * d, bytes_accessed=2**22, transcendentals=0),
        compiler_params=pltpu.CompilerParams(vmem_limit_bytes=58 * 2**20),
    )(w_cols, *pieces)


def below(rows):
    return lax.broadcasted_iota(jnp.int32, (rows, rows), 0) >= lax.broadcasted_iota(jnp.int32, (rows, rows), 1)


def inside(ready, finish, packed, scores, intra, query, key, value, upstream, states):
    rows = query.shape[0]
    for i, copy in enumerate((query, key, value, upstream, states)):
        copy[...] = packed[i * rows : i * rows + copy.shape[0], :]
    half = rows // 2
    keep = below(half)
    for s in range(2):
        place = pl.ds(s * half, half)
        got = jnp.where(keep, dot(query[place, :], key[place, :], NT), 0.0).astype(BF)
        scores[place, :] = got
        intra[place, :] = dot(got, value[place, :], NN)


def combine(ready, finish, mine, a, b, c, out):
    ready()
    d = HEAD_DIM
    total = mine[...].astype(F32) + a[...].astype(F32) + b[...].astype(F32) + c[...].astype(F32)
    out[...] = (total[:d] + total[d:]).astype(BF)


def in_parts(row):
    high = row.astype(BF).astype(F32)
    middle = (row - high).astype(BF).astype(F32)
    wide = jnp.concatenate([high, middle, row - high - middle], axis=1)
    place = lax.broadcasted_iota(jnp.int32, (16, wide.shape[1]), 0)
    return jnp.where(place == 0, wide, 0.0).astype(BF)


def states_at(mine, got, far, backward):
    d = HEAD_DIM
    place = lax.axis_index(RUN)
    total = mine[: 2 * d, :].astype(F32)
    near = jnp.zeros_like(total)
    for k, ref in enumerate(got):
        term = ref[: 2 * d, :].astype(F32)
        source = place ^ (k + 1)
        use = (source > place) if backward else (source < place)
        near = near + jnp.where(use, term, 0.0)
        total = total + term
    yh = lax.axis_index("yh")
    cross = jnp.where((yh == 0) if backward else (yh == 1), far[:d, :].astype(F32), 0.0)
    if backward:
        return near[:d] + total[d:] + cross, near[d:] + cross
    return near[:d] + cross, near[d:] + total[:d] + cross


def forward(
    ready, finish, query, intra, mine, a, b, c, far, upstream, gain, attended, mixed_grad, payload, before, gain_sum
):
    ready()
    d = HEAD_DIM
    half = query.shape[0] // 2
    scale = gain[:, pl.ds(pl.multiple_of(lax.axis_index(CUBE) * d, d), d)].astype(F32)
    gain_part = jnp.zeros((1, d), F32)
    for s, state in enumerate(states_at(mine, (a, b, c), far, False)):
        state = state.astype(BF)
        before[pl.ds(s * d, d), :] = state
        rows = pl.ds(s * half, half)
        mixed = intra[rows, :] + dot(query[rows, :], state, NN)
        inverse_rms = lax.rsqrt(jnp.mean(mixed * mixed, axis=-1, keepdims=True) + EPSILON)
        normed = mixed * inverse_rms
        attended[rows, :] = (scale * normed).astype(BF)
        up = upstream[rows, :].astype(F32)
        product = up * normed
        gain_part = gain_part + jnp.sum(product, axis=0, keepdims=True)
        along = jnp.mean(product * scale, axis=-1, keepdims=True)
        grad = (inverse_rms * (up * scale - normed * along)).astype(BF)
        mixed_grad[rows, :] = grad
        payload[pl.ds(s * d, d), :] = dot(query[rows, :], grad, TN).astype(BF)
    gain_sum[...] = jnp.broadcast_to(gain_part, gain_sum.shape)


def backward_inside(
    ready, finish, query, key, value, scores, mixed_grad, before, attended, sent, key_part, value_part
):
    ready()
    d = HEAD_DIM
    half = query.shape[0] // 2
    keep = below(half)
    for s in range(2):
        rows = pl.ds(s * half, half)
        grad = mixed_grad[rows, :]
        got = jnp.where(keep, dot(grad, value[rows, :], NT), 0.0).astype(BF)
        sent[rows, :d] = attended[rows, :]
        sent[rows, d:] = (dot(got, key[rows, :], NN) + dot(grad, before[pl.ds(s * d, d), :], NT)).astype(BF)
        key_part[rows, :] = dot(got, query[rows, :], TN)
        value_part[rows, :] = dot(scores[rows, :], grad, TN)


def backward_rest(ready, finish, key, value, sent, key_part, value_part, mine, a, b, c, far, joined, *refs):
    late, blocks = refs[:4], refs[4]
    ready()
    d = HEAD_DIM
    n = key.shape[0] // 8
    half = 4 * n
    joined[:, :d] = sent[:, d:]
    for s, state in enumerate(states_at(mine, (a, b, c), far, True)):
        state = state.astype(BF)
        rows = pl.ds(s * half, half)
        key_grad = (key_part[rows, :] + dot(value[rows, :], state, NT)).astype(BF)
        value_grad = (value_part[rows, :] + dot(key[rows, :], state, NN)).astype(BF)
        joined[rows, d : 2 * d] = key_grad
        joined[rows, 2 * d :] = value_grad
        for i in range(4):
            blocks[s * 4 + i, :, : 2 * d] = sent[pl.ds(s * half + i * n, n), :]
            blocks[s * 4 + i, :, 2 * d : 3 * d] = key_grad[i * n : (i + 1) * n]
            blocks[s * 4 + i, :, 3 * d :] = value_grad[i * n : (i + 1) * n]
    finish(0)
    chip = lax.axis_index(CUBE) // 2
    for k in range(4):
        for core in range(2):
            late[k][core] = blocks[(chip ^ k) * 2 + core]
        finish(1 + k)


def turn(pieces, width):
    n = pieces[0].shape[0]
    rows, step = 8 * n, 256

    def kernel(*refs):
        pieces, (out_far, tokens, out, sems) = refs[:8], refs[8:]
        for load in load_rows(pieces, tokens, sems):
            load.wait()
        stores = []
        for j in range(width // step):
            part = pl.ds(j * step, step)
            out[part, :] = tokens[:, j * step : (j + 1) * step].T
            stores.append(pltpu.make_async_copy(out.at[part, :], out_far.at[part, :], sems.at[8 + j]))
            stores[-1].start()
        for store in stores:
            store.wait()

    return pl.pallas_call(
        kernel,
        out_shape=pltpu.HBM((width, rows), BF),
        in_specs=[pl.BlockSpec(memory_space=pltpu.HBM)] * 8,
        out_specs=pl.BlockSpec(memory_space=pltpu.HBM),
        scratch_shapes=[
            pltpu.VMEM((rows, pieces[0].shape[1]), BF), pltpu.VMEM((width, rows), BF),
            pltpu.SemaphoreType.DMA((8 + width // step,)),
        ],
        cost_estimate=pl.CostEstimate(flops=0, bytes_accessed=2**22, transcendentals=0),
        compiler_params=pltpu.CompilerParams(vmem_limit_bytes=58 * 2**20),
    )(*pieces)


def weigh(joined, gain_sum, turned):
    width, rows = turned.shape
    d = HEAD_DIM
    step, share = 256, width // 4

    def kernel(joined_far, gain_far, turned_far, out_far, joined, gain, turned, out, sems):
        first = pltpu.make_async_copy(joined_far, joined, sems.at[0])
        second = pltpu.make_async_copy(gain_far, gain, sems.at[1])
        first.start()
        second.start()
        loads, stores = [], []
        for j in range(width // step):
            part = pl.ds(j * step, step)
            loads.append(pltpu.make_async_copy(turned_far.at[part, :], turned.at[part, :], sems.at[2 + j]))
            loads[-1].start()
        first.wait()
        second.wait()
        terms = in_parts(gain[:1, :])
        for j in range(width // step):
            loads[j].wait()
            at = j * (share + 16)
            out[at : at + share, :] = dot(turned[j * step : (j + 1) * step, :], joined[...], NN).astype(BF)
            out[at + share : at + share + 16, :] = terms
            part = pl.ds(at, share + 16)
            stores.append(pltpu.make_async_copy(out.at[part, :], out_far.at[part, :], sems.at[6 + j]))
            stores[-1].start()
        for store in stores:
            store.wait()

    return pl.pallas_call(
        kernel,
        out_shape=pltpu.HBM((width + 64, 3 * d), BF),
        in_specs=[pl.BlockSpec(memory_space=pltpu.HBM)] * 3,
        out_specs=pl.BlockSpec(memory_space=pltpu.HBM),
        scratch_shapes=[
            pltpu.VMEM((rows, 3 * d), BF), pltpu.VMEM((8, d), F32), pltpu.VMEM((width, rows), BF),
            pltpu.VMEM((width + 64, 3 * d), BF), pltpu.SemaphoreType.DMA((10,)),
        ],
        cost_estimate=pl.CostEstimate(flops=2 * rows * width * 3 * d, bytes_accessed=2**22, transcendentals=0),
        compiler_params=pltpu.CompilerParams(vmem_limit_bytes=60 * 2**20),
    )(joined, gain_sum, turned)


def at_home(ready, finish, mine, *refs):
    late, (keep, send, attended, blocks) = refs[:8], refs[8:]
    ready(*range(1, 9))
    d = HEAD_DIM
    n = attended.shape[0]
    me, core = lax.axis_index(CUBE), lax.axis_index("c")
    for k in range(HEADS):
        blocks[me ^ k, :n, :] = late[k][core]
        blocks[me ^ k, n:, :] = late[k][1 - core]
    for h in range(HEADS):
        attended[:, h * d : (h + 1) * d] = blocks[h, :n, :d]
    finish(2)
    rows = jnp.concatenate(
        [blocks[h, :, (1 + part) * d : (2 + part) * d] for part in range(3) for h in range(HEADS)], axis=1
    )
    ready(0)
    got = dot(rows, mine[...], NT).astype(BF)
    keep[...] = got[:n]
    send[...] = got[n:]


def add_first(ready, finish, pieces, out):
    ready()
    d = HEAD_DIM
    whole = pieces.shape[0] // 4
    rows = whole - 16
    total = sum(pieces[pl.ds(dp * whole, whole), :].astype(F32) for dp in range(4))
    gain = total[rows : rows + 1]
    gain = in_parts(gain[:, :d] + gain[:, d : 2 * d] + gain[:, 2 * d :])[:1, :].astype(F32)
    place = lax.broadcasted_iota(jnp.int32, (4, d), 0)
    parts = jnp.where(place == 0, gain[:, :d], jnp.where(place == 1, gain[:, d : 2 * d], gain[:, 2 * d :]))
    parts = jnp.where(place == 3, 0.0, parts)
    for j in range(rows // 4):
        four = total[j * 4 : j * 4 + 4]
        message = jnp.concatenate([four[:, :d], four[:, d : 2 * d], four[:, 2 * d :], parts], axis=0)
        out[j * 16 : j * 16 + 16, :] = message.astype(BF)


def add_up(ready, finish, pieces, keep, got, weight_grad, gain_grad, input_grad):
    ready()
    d = HEAD_DIM
    for h in range(HEADS):
        yl, low = h // 4, h % 4
        places = [((yh * 2 + yl) * 4 + run) * 4 + low for yh in range(2) for run in range(4)]
        total = sum(pieces[i * 16 : i * 16 + 16, :].astype(F32) for i in places) / 4
        for part in range(3):
            at = (part * HEADS + h) * d
            weight_grad[:, at : at + d] = total[part * 4 : part * 4 + 4]
        gain_grad[h : h + 1, :] = jnp.sum(total[12:], axis=0, keepdims=True)
    width = keep.shape[1] // 4
    even = lax.axis_index("c") == 0
    for p in range(4):
        x, y = keep[:, p * width : (p + 1) * width], got[:, p * width : (p + 1) * width]
        input_grad[:, 2 * p * width : (2 * p + 1) * width] = jnp.where(even, x, y)
        input_grad[:, (2 * p + 1) * width : (2 * p + 2) * width] = jnp.where(even, y, x)


def local(tokens, qkv_weight, out_gain, out_grad):
    replicas = lax.axis_size("dp")
    d = HEAD_DIM
    block = tokens[0]
    n, width = block.shape
    inner = out_gain.shape[0]
    depth = qkv_weight.shape[0]

    w_heads, *blocks = slices(qkv_weight, block, out_grad[0])
    near = [swap(blocks[bit], ("yl", "zl"), bit, 4) for bit in (1, 2, 3)]
    w_cols = lax.all_to_all(w_heads, "dp", 0, 0, tiled=True)
    w_half = half_rows(qkv_weight)
    mine, *_ = together(blocks[0], near[0], w_half)
    pieces = [x for side in [mine] + near for x in (side, swap(side, "c", 1, 2))]

    rows = 8 * n
    column, square = shape((rows, d), BF), shape((2 * d, d), BF)
    packed, states = project(w_cols, pieces)
    w_half, _ = together(w_half, states)
    w_mine = lax.all_gather(w_half, "dp", axis=0, tiled=True)
    got = [swap(states, RUN, bit, 4) for bit in (2, 1, 3)]
    got = [got[1], got[0], got[2]]
    scores, intra, query, key, value, upstream, states = call(
        inside, (shape((rows, rows // 2), BF), shape((rows, d), F32), column, column, column, column, square),
        packed, flops=2 * rows * rows * d, near_in=True, near_out=True, limit=12,
    )
    turned = turn(pieces, width)
    scores, turned, *got = together(scores, turned, *got)
    (both,) = call(combine, (shape((d, d), BF),), states, *got, near_in=True, near_out=True, limit=12)
    far = swap(both, "yh", 1, 2)
    attended_head, mixed_grad, payload, before, gain_sum = call(
        forward, (column, column, square, square, shape((8, d), F32)),
        query, intra, states, *got, far, upstream, out_gain.reshape(1, inner), flops=4 * rows * d * d, near_in=True, near_out=True, limit=12,
    )
    grads = [swap(payload, RUN, bit, 4) for bit in (2, 1, 3)]
    grads = [grads[1], grads[0], grads[2]]
    (both_grad,) = call(combine, (shape((d, d), BF),), payload, *grads, near_in=True, near_out=True, limit=12)
    mixed_grad, both_grad = together(mixed_grad, both_grad)
    sent, key_part, value_part = call(
        backward_inside, (shape((rows, 2 * d), BF), shape((rows, d), F32), shape((rows, d), F32)),
        query, key, value, scores, mixed_grad, before, attended_head, flops=4 * rows * rows * d, near_in=True, near_out=True, limit=12,
    )
    far_grad = swap(both_grad, "yh", 1, 2)
    joined, *late = call(
        backward_rest, (shape((rows, 3 * d), BF),) + (shape((2, n, 4 * d), BF),) * 4,
        key, value, sent, key_part, value_part, payload, *grads, far_grad, flops=8 * rows * d * d,
        near_in=True, limit=16, scratch=[pltpu.VMEM((HEADS, n, 4 * d), BF)],
    )
    late = [late[0]] + [swap(late[bit], ("yl", "zl"), bit, 4) for bit in (1, 2, 3)]
    weight_part = weigh(joined, gain_sum, turned)
    sums = lax.all_to_all(weight_part, "dp", 0, 0, tiled=True)
    (sums,) = call(add_first, (shape((width, d), BF),), sums, near_in=True, limit=12)
    first = [late[0], swap(late[0], "c", 1, 2)]
    *rest, _ = together(*late[1:], sums)
    late = first + [x for side in rest for x in (side, swap(side, "c", 1, 2))]
    sums = lax.all_to_all(sums, SEQ, 0, 0, tiled=True)
    half = shape((n, width // 2), BF)
    keep, send, attended = call(
        at_home, (half, half, shape((n, inner), BF)), w_mine, *late,
        flops=2 * n * width * 3 * inner, scratch=[pltpu.VMEM((HEADS, 2 * n, 4 * d), BF)],
    )
    got = swap(send, "c", 1, 2)
    sums, got = together(sums, got)
    weight_grad, gain_grad, input_grad = call(
        add_up, (shape((width // 256, 3 * inner), F32), shape((HEADS, d), F32), shape((n, width), BF)), sums, keep, got,
        near_in=True, limit=12,
    )
    return (attended[None], input_grad[None], weight_grad, gain_grad.reshape(inner))


def solution(mesh):
    fine = Mesh(mesh.devices.reshape(mesh.devices.shape[0], 2, 2, 2, 2, 2, 2), ALL)
    rows = P("dp", SEQ, None)
    return jax.shard_map(
        local,
        mesh=fine,
        in_specs=(rows, P("dp", None), P(), rows),
        out_specs=(rows, rows, P(ALL, None), P()),
        check_vma=False,
    )
```

```python
import jax
import jax.numpy as jnp
from jax import lax
from jax.experimental import pallas as pl
from jax.experimental.pallas import tpu as pltpu
from jax.sharding import Mesh, PartitionSpec as P

HEADS = 8
HEAD_DIM = 128
EPSILON = 1e-05
BF = jnp.bfloat16
F32 = jnp.float32

SEQ = ("yh", "yl", "zh", "zm", "zl", "c")
CUBE = ("yl", "zl", "c")
RUN = ("zh", "zm")
ALL = ("dp",) + SEQ
NN = (((1,), (0,)), ((), ()))
NT = (((1,), (1,)), ((), ()))
TN = (((0,), (0,)), ((), ()))


def swap(x, axes, bit, count):
    return lax.ppermute(x, axes, [(i, i ^ bit) for i in range(count)])


def dot(a, b, dims):
    return lax.dot_general(a, b, dims, preferred_element_type=F32)


def together(*xs):
    return lax.optimization_barrier(xs)


def call(body, outs, *operands, flops=0, scratch=(), near_in=False, near_out=False, limit=60, views=None):
    size = sum(o.size * o.dtype.itemsize for o in (*operands, *outs))
    count, total = len(operands), len(operands) + len(outs)
    moved = ([] if near_in else list(range(count))) + ([] if near_out else list(range(count, total)))
    arrays = (*operands, *outs)
    views = views or {}
    dims = [views[i][0] if i in views else x.shape for i, x in enumerate(arrays)]

    def kernel(*refs):
        given, copies, rest = refs[:total], refs[total : total + len(moved)], refs[total + len(moved) :]
        sems, rest = (rest[0], rest[1:]) if moved else (None, rest)
        slots = {i: slot for slot, i in enumerate(moved)}
        near = list(given)
        for slot, i in enumerate(moved):
            near[i] = copies[slot]
        given = [views[i][1](ref) if i in views else ref for i, ref in enumerate(given)]
        loads = {i: pltpu.make_async_copy(given[i], near[i], sems.at[slots[i]]) for i in moved if i < count}
        stores = {i - count: pltpu.make_async_copy(near[i], given[i], sems.at[slots[i]]) for i in moved if i >= count}
        waited, started = set(), set()

        def ready(*places):
            for i in places or range(count):
                if i in loads and i not in waited:
                    loads[i].wait()
                    waited.add(i)

        def finish(*places):
            for i in places or range(len(outs)):
                if i in stores and i not in started:
                    stores[i].start()
                    started.add(i)

        for load in loads.values():
            load.start()
        body(ready, finish, *near, *rest)
        ready()
        finish()
        for store in stores.values():
            store.wait()

    inside, outside = pl.BlockSpec(memory_space=pltpu.VMEM), pl.BlockSpec(memory_space=pltpu.HBM)
    return pl.pallas_call(
        kernel,
        out_shape=[o if near_out else pltpu.HBM(o.shape, o.dtype) for o in outs],
        in_specs=[inside if near_in else outside] * count,
        out_specs=[inside if near_out else outside] * len(outs),
        scratch_shapes=[pltpu.VMEM(dims[i], arrays[i].dtype) for i in moved]
        + ([pltpu.SemaphoreType.DMA((len(moved),))] if moved else [])
        + list(scratch),
        cost_estimate=pl.CostEstimate(flops=flops, bytes_accessed=size, transcendentals=0),
        compiler_params=pltpu.CompilerParams(vmem_limit_bytes=limit * 2**20),
    )(*operands)


def shape(dims, dtype):
    return jax.ShapeDtypeStruct(dims, dtype)


def slices(weight, tokens, grad):
    depth, d = weight.shape[0], HEAD_DIM
    n, width = tokens.shape

    def kernel(weight, tokens, grad, heads_out, b0, b1, b2, b3, head, tok, cols, sems):
        me = lax.axis_index(CUBE)
        loads = [(tokens, tok)]
        for k in range(4):
            at = pl.multiple_of(((me // 2) ^ k) * 2 * d, 2 * d)
            loads.append((grad.at[:, pl.ds(at, 2 * d)], cols.at[k]))
        for part in range(3):
            at = pl.multiple_of((part * HEADS + me) * d, d)
            loads.append((weight.at[:, pl.ds(at, d)], head.at[:, pl.ds(part * d, d)]))
        loads = [pltpu.make_async_copy(x, y, sems.at[i]) for i, (x, y) in enumerate(loads)]
        stores = []
        for k, block in enumerate((b0, b1, b2, b3)):
            stores.append((tok, block.at[:, pl.ds(0, width)]))
            stores.append((cols.at[k], block.at[:, pl.ds(width, 2 * d)]))
        for j in range(4):
            stores.append((head, heads_out.at[pl.ds(j * depth, depth), :]))
        stores = [pltpu.make_async_copy(x, y, sems.at[i + len(loads)]) for i, (x, y) in enumerate(stores)]
        for copy in loads:
            copy.start()
        for some, then in ((loads[:5], stores[:8]), (loads[5:], stores[8:])):
            for copy in some:
                copy.wait()
            for copy in then:
                copy.start()
        for copy in stores:
            copy.wait()

    outs = ((4 * depth, 3 * d),) + ((n, width + 2 * d),) * 4
    near = ((depth, 3 * d), (n, width), (4, n, 2 * d))
    return pl.pallas_call(
        kernel,
        out_shape=[pltpu.HBM(o, BF) for o in outs],
        in_specs=[pl.BlockSpec(memory_space=pltpu.HBM)] * 3,
        out_specs=[pl.BlockSpec(memory_space=pltpu.HBM)] * len(outs),
        scratch_shapes=[pltpu.VMEM(o, BF) for o in near] + [pltpu.SemaphoreType.DMA((20,))],
        cost_estimate=pl.CostEstimate(flops=0, bytes_accessed=2**21, transcendentals=0),
        compiler_params=pltpu.CompilerParams(vmem_limit_bytes=60 * 2**20),
    )(weight, tokens, grad)


def half_rows(weight):
    half = weight.shape[0] // 2

    def kernel(weight, out, near, sems):
        at = pl.multiple_of(lax.axis_index("c") * half, half)
        load = pltpu.make_async_copy(weight.at[pl.ds(at, half), :], near, sems.at[0])
        load.start()
        load.wait()
        store = pltpu.make_async_copy(near, out, sems.at[1])
        store.start()
        store.wait()

    return pl.pallas_call(
        kernel,
        out_shape=pltpu.HBM((half, weight.shape[1]), BF),
        in_specs=[pl.BlockSpec(memory_space=pltpu.HBM)],
        out_specs=pl.BlockSpec(memory_space=pltpu.HBM),
        scratch_shapes=[pltpu.VMEM((half, weight.shape[1]), BF), pltpu.SemaphoreType.DMA((2,))],
        cost_estimate=pl.CostEstimate(flops=0, bytes_accessed=2**21, transcendentals=0),
        compiler_params=pltpu.CompilerParams(vmem_limit_bytes=60 * 2**20),
    )(weight)


def load_rows(pieces, rows, width, sems):
    n = pieces[0].shape[0]
    me = lax.axis_index(CUBE)
    copies = []
    for k in range(8):
        place = pl.ds(pl.multiple_of((me ^ k) * n, n), n)
        copies.append(pltpu.make_async_copy(pieces[k].at[:, pl.ds(0, width)], rows.at[place, :], sems.at[k]))
        copies[-1].start()
    return copies


def project(w_cols, pieces):
    d, n = HEAD_DIM, pieces[0].shape[0]
    width, rows = w_cols.shape[0], 8 * n

    def kernel(w_far, *refs):
        pieces, (query, key, value, states, upstream, w, tokens, sems) = refs[:8], refs[8:]
        at = pl.multiple_of(width + lax.axis_index("c") * d, d)
        me = lax.axis_index(CUBE)
        first = pltpu.make_async_copy(w_far, w, sems.at[16])
        first.start()
        loads = load_rows(pieces, tokens, width, sems)
        ups = []
        for k in range(8):
            place = pl.ds(pl.multiple_of((me ^ k) * n, n), n)
            ups.append(pltpu.make_async_copy(pieces[k].at[:, pl.ds(at, d)], upstream.at[place, :], sems.at[8 + k]))
            ups[-1].start()
        first.wait()
        for load in loads:
            load.wait()
        got = dot(tokens[...], w[...], NN).astype(BF)
        for part, ref in enumerate((query, key, value)):
            ref[...] = got[:, part * d : (part + 1) * d]
        half = 4 * n
        for s in range(2):
            place = pl.ds(s * half, half)
            states[pl.ds(s * d, d), :] = dot(key[place, :], value[place, :], TN).astype(BF)
        for copy in ups:
            copy.wait()

    column = shape((rows, d), BF)
    return pl.pallas_call(
        kernel,
        out_shape=[column, column, column, shape((2 * d, d), BF), column],
        in_specs=[pl.BlockSpec(memory_space=pltpu.HBM)] * 9,
        out_specs=[pl.BlockSpec(memory_space=pltpu.VMEM)] * 5,
        scratch_shapes=[
            pltpu.VMEM(w_cols.shape, BF), pltpu.VMEM((rows, width), BF), pltpu.SemaphoreType.DMA((17,))
        ],
        cost_estimate=pl.CostEstimate(flops=2 * rows * width * 3 * d, bytes_accessed=2**22, transcendentals=0),
        compiler_params=pltpu.CompilerParams(vmem_limit_bytes=58 * 2**20),
    )(w_cols, *pieces)


def below(rows):
    return lax.broadcasted_iota(jnp.int32, (rows, rows), 0) >= lax.broadcasted_iota(jnp.int32, (rows, rows), 1)


def inside(ready, finish, query, key, value, upstream, states, scores, intra, *copies):
    for source, copy in zip((query, key, value, upstream, states), copies):
        copy[...] = source[...]
    half = query.shape[0] // 2
    keep = below(half)
    for s in range(2):
        rows = pl.ds(s * half, half)
        got = jnp.where(keep, dot(query[rows, :], key[rows, :], NT), 0.0).astype(BF)
        scores[rows, :] = got
        intra[rows, :] = dot(got, value[rows, :], NN)


def combine(ready, finish, mine, a, b, c, out):
    ready()
    d = HEAD_DIM
    total = mine[...].astype(F32) + a[...].astype(F32) + b[...].astype(F32) + c[...].astype(F32)
    out[...] = (total[:d] + total[d:]).astype(BF)


def in_parts(row):
    high = row.astype(BF).astype(F32)
    middle = (row - high).astype(BF).astype(F32)
    wide = jnp.concatenate([high, middle, row - high - middle], axis=1)
    place = lax.broadcasted_iota(jnp.int32, (16, wide.shape[1]), 0)
    return jnp.where(place == 0, wide, 0.0).astype(BF)


def states_at(mine, got, far, backward):
    d = HEAD_DIM
    place = lax.axis_index(RUN)
    total = mine[: 2 * d, :].astype(F32)
    near = jnp.zeros_like(total)
    for k, ref in enumerate(got):
        term = ref[: 2 * d, :].astype(F32)
        source = place ^ (k + 1)
        use = (source > place) if backward else (source < place)
        near = near + jnp.where(use, term, 0.0)
        total = total + term
    yh = lax.axis_index("yh")
    cross = jnp.where((yh == 0) if backward else (yh == 1), far[:d, :].astype(F32), 0.0)
    if backward:
        return near[:d] + total[d:] + cross, near[d:] + cross
    return near[:d] + cross, near[d:] + total[:d] + cross


def forward(
    ready, finish, query, intra, mine, a, b, c, far, upstream, gain, attended, mixed_grad, payload, before, gain_sum
):
    ready()
    d = HEAD_DIM
    half = query.shape[0] // 2
    scale = gain[:, pl.ds(pl.multiple_of(lax.axis_index(CUBE) * d, d), d)].astype(F32)
    gain_part = jnp.zeros((1, d), F32)
    for s, state in enumerate(states_at(mine, (a, b, c), far, False)):
        state = state.astype(BF)
        before[pl.ds(s * d, d), :] = state
        rows = pl.ds(s * half, half)
        mixed = intra[rows, :] + dot(query[rows, :], state, NN)
        inverse_rms = lax.rsqrt(jnp.mean(mixed * mixed, axis=-1, keepdims=True) + EPSILON)
        normed = mixed * inverse_rms
        attended[rows, :] = (scale * normed).astype(BF)
        up = upstream[rows, :].astype(F32)
        product = up * normed
        gain_part = gain_part + jnp.sum(product, axis=0, keepdims=True)
        along = jnp.mean(product * scale, axis=-1, keepdims=True)
        grad = (inverse_rms * (up * scale - normed * along)).astype(BF)
        mixed_grad[rows, :] = grad
        payload[pl.ds(s * d, d), :] = dot(query[rows, :], grad, TN).astype(BF)
    gain_sum[...] = jnp.broadcast_to(gain_part, gain_sum.shape)


def backward_inside(
    ready, finish, query, key, value, scores, mixed_grad, before, attended, sent, key_part, value_part
):
    ready()
    d = HEAD_DIM
    half = query.shape[0] // 2
    keep = below(half)
    for s in range(2):
        rows = pl.ds(s * half, half)
        grad = mixed_grad[rows, :]
        got = jnp.where(keep, dot(grad, value[rows, :], NT), 0.0).astype(BF)
        sent[rows, :d] = attended[rows, :]
        sent[rows, d:] = (dot(got, key[rows, :], NN) + dot(grad, before[pl.ds(s * d, d), :], NT)).astype(BF)
        key_part[rows, :] = dot(got, query[rows, :], TN)
        value_part[rows, :] = dot(scores[rows, :], grad, TN)


def backward_rest(ready, finish, key, value, sent, key_part, value_part, mine, a, b, c, far, joined, *refs):
    late, blocks = refs[:4], refs[4]
    ready()
    d = HEAD_DIM
    n = key.shape[0] // 8
    half = 4 * n
    joined[:, :d] = sent[:, d:]
    for s, state in enumerate(states_at(mine, (a, b, c), far, True)):
        state = state.astype(BF)
        rows = pl.ds(s * half, half)
        key_grad = (key_part[rows, :] + dot(value[rows, :], state, NT)).astype(BF)
        value_grad = (value_part[rows, :] + dot(key[rows, :], state, NN)).astype(BF)
        joined[rows, d : 2 * d] = key_grad
        joined[rows, 2 * d :] = value_grad
        for i in range(4):
            blocks[s * 4 + i, :, : 2 * d] = sent[pl.ds(s * half + i * n, n), :]
            blocks[s * 4 + i, :, 2 * d : 3 * d] = key_grad[i * n : (i + 1) * n]
            blocks[s * 4 + i, :, 3 * d :] = value_grad[i * n : (i + 1) * n]
    finish(0)
    chip = lax.axis_index(CUBE) // 2
    for k in range(4):
        for core in range(2):
            late[k][core] = blocks[(chip ^ k) * 2 + core]
        finish(1 + k)


def weigh(joined, gain_sum, pieces, width):
    n, d = pieces[0].shape[0], HEAD_DIM
    rows = 8 * n

    def kernel(joined_far, gain_far, *refs):
        pieces, (out_far, joined, gain, tokens, out, sems) = refs[:8], refs[8:]
        first = pltpu.make_async_copy(joined_far, joined, sems.at[8])
        second = pltpu.make_async_copy(gain_far, gain, sems.at[10])
        first.start()
        second.start()
        loads = load_rows(pieces, tokens, width, sems)
        first.wait()
        for load in loads:
            load.wait()
        second.wait()
        terms = in_parts(gain[:1, :])
        step, share = 256, width // 4
        for j in range(width // step):
            got = dot(tokens[:, j * step : (j + 1) * step].T, joined[...], NN).astype(BF)
            for i in range(step // share):
                at = (j * (step // share) + i) * (share + 16)
                out[at : at + share, :] = got[i * share : (i + 1) * share]
                out[at + share : at + share + 16, :] = terms
        last = pltpu.make_async_copy(out, out_far, sems.at[9])
        last.start()
        last.wait()

    return pl.pallas_call(
        kernel,
        out_shape=pltpu.HBM((width + 64, 3 * d), BF),
        in_specs=[pl.BlockSpec(memory_space=pltpu.HBM)] * 10,
        out_specs=pl.BlockSpec(memory_space=pltpu.HBM),
        scratch_shapes=[
            pltpu.VMEM((rows, 3 * d), BF), pltpu.VMEM((8, d), F32), pltpu.VMEM((rows, width), BF),
            pltpu.VMEM((width + 64, 3 * d), BF), pltpu.SemaphoreType.DMA((11,)),
        ],
        cost_estimate=pl.CostEstimate(flops=2 * rows * width * 3 * d, bytes_accessed=2**22, transcendentals=0),
        compiler_params=pltpu.CompilerParams(vmem_limit_bytes=60 * 2**20),
    )(joined, gain_sum, *pieces)


def at_home(ready, finish, mine, *refs):
    late, (keep, send, attended, blocks) = refs[:8], refs[8:]
    ready(*range(1, 9))
    d = HEAD_DIM
    n = attended.shape[0]
    me, core = lax.axis_index(CUBE), lax.axis_index("c")
    for k in range(HEADS):
        blocks[me ^ k, :n, :] = late[k][core]
        blocks[me ^ k, n:, :] = late[k][1 - core]
    for h in range(HEADS):
        attended[:, h * d : (h + 1) * d] = blocks[h, :n, :d]
    finish(2)
    rows = jnp.concatenate(
        [blocks[h, :, (1 + part) * d : (2 + part) * d] for part in range(3) for h in range(HEADS)], axis=1
    )
    ready(0)
    got = dot(rows, mine[...], NT).astype(BF)
    keep[...] = got[:n]
    send[...] = got[n:]


def add_first(ready, finish, pieces, out):
    ready()
    d = HEAD_DIM
    whole = pieces.shape[0] // 4
    rows = whole - 16
    total = sum(pieces[pl.ds(dp * whole, whole), :].astype(F32) for dp in range(4))
    gain = total[rows : rows + 1]
    gain = in_parts(gain[:, :d] + gain[:, d : 2 * d] + gain[:, 2 * d :])[:1, :].astype(F32)
    place = lax.broadcasted_iota(jnp.int32, (4, d), 0)
    parts = jnp.where(place == 0, gain[:, :d], jnp.where(place == 1, gain[:, d : 2 * d], gain[:, 2 * d :]))
    parts = jnp.where(place == 3, 0.0, parts)
    for j in range(rows // 4):
        four = total[j * 4 : j * 4 + 4]
        message = jnp.concatenate([four[:, :d], four[:, d : 2 * d], four[:, 2 * d :], parts], axis=0)
        out[j * 16 : j * 16 + 16, :] = message.astype(BF)


def add_second(ready, finish, pieces, out):
    ready()
    rows = pieces.shape[0] // 4
    for yl in range(2):
        total = pieces[yl * rows : (yl + 1) * rows, :].astype(F32) + pieces[
            (2 + yl) * rows : (3 + yl) * rows, :
        ].astype(F32)
        for j in range(16):
            out[j * 32 + yl * 16 : j * 32 + yl * 16 + 16, :] = total[j * 16 : j * 16 + 16]


def add_up(ready, finish, pieces, keep, got, weight_grad, gain_grad, input_grad):
    ready()
    d = HEAD_DIM
    for h in range(HEADS):
        yl, low = h // 4, h % 4
        places = [(run * 4 + low) * 32 + yl * 16 for run in range(4)]
        total = sum(pieces[at : at + 16, :] for at in places) / 4
        for part in range(3):
            at = (part * HEADS + h) * d
            weight_grad[:, at : at + d] = total[part * 4 : part * 4 + 4]
        gain_grad[h : h + 1, :] = jnp.sum(total[12:], axis=0, keepdims=True)
    width = keep.shape[1] // 4
    even = lax.axis_index("c") == 0
    for p in range(4):
        x, y = keep[:, p * width : (p + 1) * width], got[:, p * width : (p + 1) * width]
        input_grad[:, 2 * p * width : (2 * p + 1) * width] = jnp.where(even, x, y)
        input_grad[:, (2 * p + 1) * width : (2 * p + 2) * width] = jnp.where(even, y, x)


def local(tokens, qkv_weight, out_gain, out_grad):
    replicas = lax.axis_size("dp")
    d = HEAD_DIM
    block = tokens[0]
    n, width = block.shape
    inner = out_gain.shape[0]
    depth = qkv_weight.shape[0]

    w_heads, *blocks = slices(qkv_weight, block, out_grad[0])
    near = [swap(blocks[bit], ("yl", "zl"), bit, 4) for bit in (1, 2, 3)]
    w_cols = lax.all_to_all(w_heads, "dp", 0, 0, tiled=True)
    w_half = half_rows(qkv_weight)
    mine, *_ = together(blocks[0], near[0], w_half)
    pieces = [x for side in [mine] + near for x in (side, swap(side, "c", 1, 2))]

    rows = 8 * n
    column, square = shape((rows, d), BF), shape((2 * d, d), BF)
    query, key, value, states, upstream = project(w_cols, pieces)
    w_half, _ = together(w_half, states)
    w_mine = lax.all_gather(w_half, "dp", axis=0, tiled=True)
    got = [swap(states, RUN, bit, 4) for bit in (1, 2, 3)]
    scores, intra, query, key, value, upstream, states = call(
        inside, (shape((rows, rows // 2), BF), shape((rows, d), F32), column, column, column, column, square),
        query, key, value, upstream, states, flops=2 * rows * rows * d, near_in=True, near_out=True, limit=12,
    )
    scores, *got = together(scores, *got)
    (both,) = call(combine, (shape((d, d), BF),), states, *got, near_in=True, near_out=True, limit=12)
    far = swap(both, "yh", 1, 2)
    attended_head, mixed_grad, payload, before, gain_sum = call(
        forward, (column, column, square, square, shape((8, d), F32)),
        query, intra, states, *got, far, upstream, out_gain.reshape(1, inner), flops=4 * rows * d * d, near_in=True, near_out=True, limit=12,
    )
    grads = [swap(payload, RUN, bit, 4) for bit in (1, 2, 3)]
    (both_grad,) = call(combine, (shape((d, d), BF),), payload, *grads, near_in=True, near_out=True, limit=12)
    mixed_grad, both_grad = together(mixed_grad, both_grad)
    sent, key_part, value_part = call(
        backward_inside, (shape((rows, 2 * d), BF), shape((rows, d), F32), shape((rows, d), F32)),
        query, key, value, scores, mixed_grad, before, attended_head, flops=4 * rows * rows * d, near_in=True, near_out=True, limit=12,
    )
    far_grad = swap(both_grad, "yh", 1, 2)
    joined, *late = call(
        backward_rest, (shape((rows, 3 * d), BF),) + (shape((2, n, 4 * d), BF),) * 4,
        key, value, sent, key_part, value_part, payload, *grads, far_grad, flops=8 * rows * d * d,
        near_in=True, limit=16, scratch=[pltpu.VMEM((HEADS, n, 4 * d), BF)],
    )
    late = [late[0]] + [swap(late[bit], ("yl", "zl"), bit, 4) for bit in (1, 2, 3)]
    weight_part = weigh(joined, gain_sum, pieces, width)
    sums = lax.all_to_all(weight_part, "dp", 0, 0, tiled=True)
    (sums,) = call(add_first, (shape((width, d), BF),), sums, near_in=True, limit=12)
    *late, _ = together(*late, sums)
    late = [x for side in late for x in (side, swap(side, "c", 1, 2))]
    sums = lax.all_to_all(sums, ("yh", "yl"), 0, 0, tiled=True)
    (sums,) = call(add_second, (shape((width // 2, d), F32),), sums, near_in=True, limit=12)
    sums = lax.all_to_all(sums, ("zh", "zm", "zl", "c"), 0, 0, tiled=True)
    half = shape((n, width // 2), BF)
    keep, send, attended = call(
        at_home, (half, half, shape((n, inner), BF)), w_mine, *late,
        flops=2 * n * width * 3 * inner, scratch=[pltpu.VMEM((HEADS, 2 * n, 4 * d), BF)],
    )
    got = swap(send, "c", 1, 2)
    sums, got = together(sums, got)
    weight_grad, gain_grad, input_grad = call(
        add_up, (shape((width // 256, 3 * inner), F32), shape((HEADS, d), F32), shape((n, width), BF)), sums, keep, got,
        near_in=True, limit=12,
    )
    return (attended[None], input_grad[None], weight_grad, gain_grad.reshape(inner))


def solution(mesh):
    fine = Mesh(mesh.devices.reshape(mesh.devices.shape[0], 2, 2, 2, 2, 2, 2), ALL)
    rows = P("dp", SEQ, None)
    return jax.shard_map(
        local,
        mesh=fine,
        in_specs=(rows, P("dp", None), P(), rows),
        out_specs=(rows, rows, P(ALL, None), P()),
        check_vma=False,
    )
```
